512 devices in a mesh: group: 8 (over z_lo), member: 64 (over x, y, z_hi, core).
Axes of the slice: x: 4, y: 4, z: 16 (z_hi: 2, z_lo: 8; z = z_hi * 8 + z_lo), core: 2. Of those that a mesh axis runs over, the one named last changes fastest.
Arguments:
- embeddings: bfloat16 [262144, 1024], P(('group', 'member')), may hold values from -6 to 6
- assign: int32 [262144], P(('group', 'member')), may hold values from 0 to 255, as said below
- cluster_list: int32 [512, 64], P(('group', 'member')), may hold values from 0 to 255, as said below
- owner_map: int32 [8, 256], P('group'), may hold values from 0 to 255, as said below
- old_centroids: float32 [2048, 1024], P(('group', 'member')), may hold values from -16 to 16
Outputs:
- centroids: bfloat16 [2048, 1024], P(('group', 'member'))
- block_max: float32 [262144, 512], P(('group', 'member'))
The draws below stay inside these ranges and needn't reach their ends.
Inputs may be any that keep to these rules, and one draw needn't show every extreme that they name: Each row of owner_map is a permutation; the centroid at position p of group g is row g * 256 + p of old_centroids and centroids. `cluster_list`: each device lists 64 distinct clusters of its group's slab. Of the 4 clusters whose positions p share p // 4, a device lists at most 2, and every device lists exactly 2 of some such set. `assign`: A cluster number within the slab of the row's group.
All inputs are finite; a program needn't handle non-finite values.
Results may differ from the reference program's by a relative error of at most 0.0023.
Values may be sent and summed in bfloat16 or wider, within the bound.
A program may use at most 64 MiB of HBM per device.

```python
import math
import jax
import jax.numpy as jnp
from jax import lax

D = 1024
KC = 4
CAP = 2
ROWS_DEV = 512
SLAB = 256
LIST = 64
K = 2048
ROWS = 262144
N_GROUP = 8
N_MEMBER = 64


def shared_layout(key):
    key = jax.random.fold_in(key, 7)
    keys = jax.random.split(key, 8)
    devices_all = N_GROUP * N_MEMBER
    permutations = jax.vmap(lambda subkey: jax.random.permutation(subkey, SLAB))(jax.random.split(keys[0], N_GROUP)).astype(jnp.int32)
    inverse = jnp.argsort(permutations, axis=1).astype(jnp.int32)
    within = jax.random.randint(keys[1], (devices_all, N_MEMBER, KC), 0, 1 << 16) * KC + jnp.arange(KC, dtype=jnp.int32)
    larger = jnp.sum((within[..., None, :] > within[..., :, None]).astype(jnp.int32), axis=-1)
    allowed = (larger < CAP).reshape(devices_all, SLAB).astype(jnp.int32)
    forced_member = jax.random.randint(keys[2], (devices_all, 1), 0, N_MEMBER)
    forced = (jnp.arange(SLAB, dtype=jnp.int32)[None, :] // KC == forced_member).astype(jnp.int32)
    picking = jax.random.randint(keys[3], (devices_all, SLAB), 0, 1 << 16) * SLAB + jnp.arange(SLAB, dtype=jnp.int32)
    ranking = allowed * (1 << 29) + allowed * forced * (1 << 28) + picking
    _, positions = lax.top_k(ranking, LIST)
    shuffle = jax.random.randint(keys[4], (devices_all, LIST), 0, 1 << 16) * LIST + jnp.arange(LIST, dtype=jnp.int32)
    positions = jnp.take_along_axis(positions.astype(jnp.int32), jnp.argsort(shuffle, axis=1).astype(jnp.int32), axis=1)
    group_of = jnp.arange(devices_all, dtype=jnp.int32) // N_MEMBER
    listing = jnp.take_along_axis(inverse[group_of], positions, axis=1).astype(jnp.int32)
    choose = jax.random.randint(keys[5], (devices_all, ROWS_DEV), 0, LIST)
    from_list = jnp.take_along_axis(listing, choose, axis=1)
    anywhere = jax.random.randint(keys[6], (devices_all, ROWS_DEV), 0, SLAB)
    use_list = jax.random.randint(keys[7], (devices_all, ROWS_DEV), 0, 4) < 3
    assigned = jnp.where(use_list, from_list, anywhere).astype(jnp.int32).reshape(devices_all * ROWS_DEV)
    return (permutations, listing, assigned)


def draw_assign(key, part):
    return shared_layout(key)[2]


def draw_cluster_list(key, part):
    return shared_layout(key)[1]


def draw_owner_map(key, part):
    return shared_layout(key)[0]


def steps_of(rng, shape, pieces, low, top_value):
    gain = 1.0
    for dim, blocks in pieces:
        steps = jax.random.uniform(jax.random.fold_in(jax.random.fold_in(rng, 6), dim), (blocks,), jnp.float32, low / len(pieces), top_value / len(pieces))
        gain = gain * jnp.repeat(jnp.exp(steps), shape[dim] // blocks).reshape((-1,) + (1,) * (len(shape) - 1 - dim))
    return gain


def gaussian(key, extent, width, limit, cuts=(), kind=jnp.bfloat16):
    level = steps_of(key, extent, cuts, -0.22, 0.18) if cuts else 1.0
    result = jax.random.normal(key, extent, jnp.float32) * width * level
    return jnp.minimum(jnp.maximum(result, -limit), limit).astype(kind)


def setup_inputs(seed: int = 0) -> dict:
    seeds = jax.random.split(jax.random.key(seed), 6)
    return {
        "embeddings": gaussian(seeds[0], (ROWS, D), 1.0, 6.0, ((0, 512),)),
        "assign": draw_assign(jax.random.fold_in(seeds[5], 71), 0),
        "cluster_list": draw_cluster_list(jax.random.fold_in(seeds[5], 71), 0),
        "owner_map": draw_owner_map(jax.random.fold_in(seeds[5], 71), 0),
        "old_centroids": gaussian(seeds[4], (K, D), 3.0, 16.0, ((0, 512),), jnp.float32),
    }


def reference(embeddings, assign, cluster_list, owner_map, old_centroids):
    devices_all = N_GROUP * N_MEMBER
    dev_index = jnp.arange(devices_all, dtype=jnp.int32)[:, None]
    marked = jnp.zeros((devices_all, SLAB), jnp.int32).at[dev_index, cluster_list].set(1)
    assigned = assign.reshape(devices_all, ROWS_DEV)
    kept = jnp.take_along_axis(marked, assigned, axis=1)
    owners = jnp.repeat(owner_map, N_MEMBER, axis=0)
    position = jnp.take_along_axis(owners, assigned, axis=1)
    position = jnp.where(kept > 0, position, SLAB).astype(jnp.int32).reshape(N_GROUP, N_MEMBER * ROWS_DEV)
    grouped = embeddings.reshape(N_GROUP, N_MEMBER * ROWS_DEV, D)
    prior = old_centroids.reshape(N_GROUP, SLAB, D)

    def update(operands):
        row_block, target, previous = operands
        cluster_sums = jax.ops.segment_sum(row_block.astype(jnp.float32), target, num_segments=SLAB + 1)[:SLAB]
        counts = jax.ops.segment_sum(jnp.ones(target.shape, jnp.float32), target, num_segments=SLAB + 1)[:SLAB]
        updated = (cluster_sums + previous) / (counts + 1.0)[:, None]
        normed = updated * lax.rsqrt(lax.optimization_barrier(jnp.mean(updated * updated, axis=1, keepdims=True)) + 1e-05)
        return normed.astype(jnp.bfloat16)
    centroids = lax.map(update, (grouped, position, prior)).reshape(N_GROUP * SLAB, D)
    centre_wide = centroids.astype(jnp.float32)
    inverse_root = 1.0 / math.sqrt(D)

    def row_tile(row_block):
        similarity = jnp.dot(row_block.astype(jnp.float32), centre_wide.T, precision=lax.Precision.HIGHEST) * inverse_root
        return lax.optimization_barrier(jnp.max(similarity.reshape(ROWS_DEV, N_GROUP * SLAB // KC, KC), axis=2))
    block_max = lax.map(row_tile, embeddings.reshape(devices_all, ROWS_DEV, D))
    block_max = block_max.reshape(devices_all * ROWS_DEV, N_GROUP * SLAB // KC)
    return (centroids, block_max)
```

```python
import math

import jax
import jax.numpy as jnp
from jax import lax
from jax.experimental import pallas as pl
from jax.experimental.pallas import tpu as pltpu
from jax.sharding import PartitionSpec as P

F32, BF16, I32 = jnp.float32, jnp.bfloat16, jnp.int32
MSG = 640
OFFSETS = (0, 1, -1, 2, -2, 3, -3, 4)


def iota(shape, dim):
    return lax.broadcasted_iota(I32, shape, dim)


def split3(v):
    hi = v.astype(BF16)
    rest = v - hi.astype(F32)
    mid = rest.astype(BF16)
    low = (rest - mid.astype(F32)).astype(BF16)
    return hi, mid, low


def column_of(row, n):
    eye = iota((n, n), 0) == iota((n, n), 1)
    return jnp.sum(jnp.where(eye, row, 0), axis=1, keepdims=True)


def row_of(col, n):
    eye = iota((n, n), 0) == iota((n, n), 1)
    return jnp.sum(jnp.where(eye, col, 0), axis=0, keepdims=True)


def slot_rows(list_row, pos_row):
    lists = list_row.shape[1]
    listed = jnp.max(
        jnp.where(list_row == iota((256, lists), 0), 1, 0), axis=1, keepdims=True
    )
    pos_col = column_of(pos_row, 256)
    key = jnp.where(listed > 0, pos_col, -8)
    rank = jnp.sum(
        jnp.where(((key >> 2) == (pos_row >> 2)) & (key < pos_row), 1, 0), axis=0, keepdims=True
    )
    listed_row = row_of(listed, 256)
    chip = pos_row >> 4
    core = (pos_row >> 2) & 1
    high = (pos_row >> 3) & 1
    turned = ((chip & 3) << 2) | (chip >> 2)
    target = core * 16 + jnp.where(core == 0, chip, turned)
    slot = jnp.where(listed_row > 0, target * 4 + high * 2 + rank + 1, 0)
    return slot, high * 4 + (pos_row & 3)


def kernel(
    emb, assign, listing, owner, old, cent_out, out,
    perm, send, recv, zsend, zrecv, raw, slab,
    a2a_send, a2a_recv, zx_send, zx_recv, ag_send, z_recv, step_recv,
):
    g = lax.axis_index("group")
    m = lax.axis_index("member")
    x, y, zh, c = m // 16, (m // 4) % 4, (m // 2) % 2, m % 2
    z = zh * 8 + g
    a = jnp.where(c == 0, y, x)
    b = jnp.where(c == 0, x, y)
    me = c * 16 + b * 4 + a

    def at_plane(core, bb, aa):
        xx = jnp.where(core == 0, bb, aa)
        yy = jnp.where(core == 0, aa, bb)
        return {"member": xx * 16 + yy * 4 + zh * 2 + core}

    def at_z(zz):
        zz = (zz + 16) % 16
        return {"group": zz % 8, "member": x * 16 + y * 4 + (zz // 8) * 2 + c}

    def plane_peer(i):
        t = (me + i) % 32
        return t, at_plane(t // 16, (t // 4) % 4, t % 4)

    barrier = pltpu.get_barrier_semaphore()

    def greet(i, carry):
        pl.semaphore_signal(barrier, inc=1, device_id=plane_peer(i)[1])
        return carry

    lax.fori_loop(1, 32, greet, 0)
    for d in (1, -1, 2, -2, 3, -3, 4, -4, 8):
        pl.semaphore_signal(barrier, inc=1, device_id=at_z(z + d))

    slot_row, line_row = slot_rows(listing[...], owner[...])
    slot_col = column_of(slot_row, 256)
    row_slot = jnp.sum(
        jnp.where(assign[...] == iota((256, 512), 0), slot_col, 0), axis=0, keepdims=True
    )
    index = iota((256, 1), 0)
    half = (index >> 2) & 1
    wanted = ((index >> 3) << 2 | (index & 3)) + 1
    member_of = row_slot == wanted
    member_f = jnp.where(member_of, 1.0, 0.0)
    count = jnp.sum(member_f, axis=1, keepdims=True)
    member_b = member_f.astype(BF16)
    line = jnp.sum(jnp.where(slot_row == wanted, line_row + 1, 0), axis=1, keepdims=True) - 1
    lane = iota((256, 128), 1)
    mark = jnp.where(((lane & 7) == line) & ((lane >> 3) == half), 1.0, 0.0)
    send[:, 512:] = jnp.where(lane < 16, mark, count)
    for col in range(0, 512, 256):
        low = jnp.dot(member_b, emb[:, col:col + 256], preferred_element_type=F32)
        high = jnp.dot(member_b, emb[:, 512 + col:512 + col + 256], preferred_element_type=F32)
        send[:, col:col + 256] = jnp.where(half == 0, low, high)

    pl.semaphore_wait(barrier, 40)

    def give(i, carry):
        t, peer = plane_peer(i)
        pltpu.make_async_remote_copy(
            src_ref=send.at[pl.ds(pl.multiple_of(t * 8, 8), 8)],
            dst_ref=recv.at[pl.ds(pl.multiple_of(me * 8, 8), 8)],
            send_sem=a2a_send,
            recv_sem=a2a_recv,
            device_id=peer,
        ).start()
        return carry

    lax.fori_loop(1, 32, give, 0)
    mine = pl.ds(pl.multiple_of(me * 8, 8), 8)
    recv[mine, :] = send[mine, :]

    k = iota((1, 512), 1)
    kc, kb, ka = k >> 8, (k >> 6) & 3, (k >> 4) & 3
    block = jnp.where(kc == 0, kb * 4 + ka, ka * 4 + kb) * 4 + ((k >> 2) & 1) * 2 + kc
    goal = ((k >> 3) & 1) * 256 + (k & 3) * 64 + block
    perm[...] = jnp.where(goal == iota((512, 512), 0), 1.0, 0.0).astype(BF16)
    out[...] = jnp.zeros_like(out)

    def all_but_one(src, dst, ssem, rsem, peer):
        return pltpu.make_async_remote_copy(
            src_ref=src.at[pl.ds(0, 248)], dst_ref=dst.at[pl.ds(0, 248)],
            send_sem=ssem, recv_sem=rsem, device_id=peer,
        )

    whole = all_but_one(send, recv, a2a_send, a2a_recv, plane_peer(1)[1])
    whole.wait_recv()
    marks = jnp.where(lane < 16, recv[:, 512:], 0.0).astype(BF16)
    total = None
    for part in split3(recv[...]):
        term = lax.dot_general(
            marks, part, (((0,), (0,)), ((), ())), preferred_element_type=F32
        )[:16]
        total = term if total is None else total + term
    line16 = iota((16, 1), 0) & 7
    prior = jnp.zeros((16, 512), F32)
    upper = iota((16, 1), 0) >= 8
    for j in range(4):
        rows = jnp.where(upper, old[j:j + 1, 512:], old[j:j + 1, :512])
        prior = prior + jnp.where(line16 == zh * 4 + j, rows, 0.0)
    zsend[:, :512] = total[:, :512] + prior
    zsend[:, 512:] = total[:, 512:]
    across = pltpu.make_async_remote_copy(
        src_ref=zsend, dst_ref=zrecv, send_sem=zx_send, recv_sem=zx_recv, device_id=at_z(z + 8)
    )
    across.start()
    across.wait_recv()
    tally = zsend[:, 512 + 16:512 + 17] + zrecv[:, 512 + 16:512 + 17]
    updated = (zsend[:, :512] + zrecv[:, :512]) / (tally + 1.0)
    squares = jnp.sum(updated * updated, axis=1, keepdims=True)
    mean = (squares[:8] + squares[8:]) * (1.0 / 1024)
    scale = lax.rsqrt(mean + 1e-05)
    cent = updated * jnp.concatenate([scale, scale], axis=0)
    for h in range(2):
        part = cent[8 * h:8 * h + 8]
        cent_out[:, 512 * h:512 * h + 512] = jnp.where(zh == 0, part[:4], part[4:]).astype(BF16)

    def at_row(gg, bb, aa):
        return pl.multiple_of((((c * 8 + gg) * 4 + bb) * 4 + aa) * 16, 16)

    raw[pl.ds(at_row(g, b, a), 16), :] = cent.astype(BF16)

    def copy(row, rows, sem, peer, cols=None):
        ref = raw.at[pl.ds(row, rows)] if cols is None else raw.at[pl.ds(row, rows), cols]
        return pltpu.make_async_remote_copy(
            src_ref=ref, dst_ref=ref, send_sem=ag_send, recv_sem=sem, device_id=peer
        )

    for n in range(1, 8):
        copy(at_row(g, b, a), 16, z_recv.at[n], at_z(z - OFFSETS[n])).start()

    left, right = (a + 3) % 4, (a + 1) % 4
    down, up = (b + 3) % 4, (b + 1) % 4
    far_a, far_b = (a + 2) % 4, (b + 2) % 4
    to_left, to_right = at_plane(c, b, left), at_plane(c, b, right)
    to_down, to_up = at_plane(c, down, a), at_plane(c, up, a)
    sibling = {"member": m + 1 - 2 * c}
    lo, hi = pl.ds(0, 256), pl.ds(256, 256)

    def group_of(n):
        offset = jnp.where(n % 2 == 1, (n + 1) // 2, -(n // 2))
        return (z + offset + 16) % 8

    def stage_z(n):
        gg = group_of(n)

        @pl.when(n > 0)
        def _():
            copy(at_row(gg, b, a), 16, z_recv.at[n], sibling).wait_recv()

        copy(at_row(gg, b, a), 16, step_recv.at[0, n], to_right).start()
        copy(at_row(gg, b, a), 16, step_recv.at[1, n], to_left).start()

    def stage_a(n):
        gg = group_of(n)
        copy(at_row(gg, b, left), 16, step_recv.at[0, n], to_right).wait_recv()
        copy(at_row(gg, b, left), 16, step_recv.at[2, n], to_right, lo).start()
        copy(at_row(gg, b, right), 16, step_recv.at[1, n], to_left).wait_recv()
        copy(at_row(gg, b, right), 16, step_recv.at[3, n], to_left, hi).start()

    def stage_a_far(n):
        gg = group_of(n)
        copy(at_row(gg, b, far_a), 16, step_recv.at[2, n], to_right, lo).wait_recv()
        copy(at_row(gg, b, far_a), 16, step_recv.at[3, n], to_left, hi).wait_recv()
        copy(at_row(gg, b, 0), 64, step_recv.at[4, n], to_up).start()
        copy(at_row(gg, b, 0), 64, step_recv.at[5, n], to_down).start()

    def stage_b(n):
        gg = group_of(n)
        copy(at_row(gg, down, 0), 64, step_recv.at[4, n], to_up).wait_recv()
        copy(at_row(gg, down, 0), 32, step_recv.at[6, n], to_up).start()
        copy(at_row(gg, up, 0), 64, step_recv.at[5, n], to_down).wait_recv()
        copy(at_row(gg, up, 2), 32, step_recv.at[7, n], to_down).start()

    def stage_b_far(n):
        gg = group_of(n)
        copy(at_row(gg, far_b, 0), 32, step_recv.at[6, n], to_up).wait_recv()
        copy(at_row(gg, far_b, 2), 32, step_recv.at[7, n], to_down).wait_recv()
        copy(at_row(gg, 0, 0), 256, step_recv.at[8, n], sibling).start()

    def stage_dot(n):
        gg = group_of(n)
        theirs = pl.multiple_of(((1 - c) * 8 + gg) * 256, 256)
        pltpu.make_async_remote_copy(
            src_ref=raw.at[pl.ds(theirs, 256)], dst_ref=raw.at[pl.ds(theirs, 256)],
            send_sem=ag_send, recv_sem=step_recv.at[8, n], device_id=sibling,
        ).wait_recv()
        first = raw[pl.ds(pl.multiple_of(gg * 256, 256), 256), :]
        second = raw[pl.ds(pl.multiple_of((8 + gg) * 256, 256), 256), :]
        for h in range(2):
            rows = slice(256 * h, 256 * h + 256)
            turned = jnp.dot(perm[rows, :256], first, preferred_element_type=F32)
            turned = turned + jnp.dot(perm[rows, 256:], second, preferred_element_type=F32)
            slab[:, 512 * h:512 * h + 512] = turned.astype(BF16)
        lanes = pl.ds(pl.multiple_of((gg // 2) * 128, 128), 128)
        for r in range(0, 512, 256):
            sim = lax.dot_general(
                emb[r:r + 256, :], slab[...], (((1,), (1,)), ((), ())), preferred_element_type=F32
            )
            best = jnp.maximum(sim[:, :128], sim[:, 128:])
            best = jnp.maximum(best, pltpu.roll(best, 64, 1)) * (1.0 / math.sqrt(1024))
            keep = (iota((256, 128), 1) >> 6) == gg % 2
            out[r:r + 256, lanes] = jnp.where(keep, best, out[r:r + 256, lanes])

    stages = (stage_z, stage_a, stage_a_far, stage_b, stage_b_far, stage_dot)

    def tick(i, carry):
        for lag, stage in enumerate(stages):
            n = i - lag

            @pl.when((n >= 0) & (n < 8))
            def _(stage=stage, n=n):
                stage(n)

        return carry

    lax.fori_loop(0, 8 + len(stages) - 1, tick, 0)

    whole.wait_send()
    across.wait_send()
    sent = 7 * 16 + 8 * (32 + 16) + 8 * (128 + 64) + 8 * 256
    pltpu.make_async_remote_copy(
        src_ref=raw.at[pl.ds(0, sent)], dst_ref=raw.at[pl.ds(0, sent)],
        send_sem=ag_send, recv_sem=z_recv.at[0], device_id=sibling,
    ).wait_send()


def shards(embeddings, assign, cluster_list, owner_map, old_centroids):
    vmem = pl.BlockSpec(memory_space=pltpu.VMEM)
    return pl.pallas_call(
        kernel,
        out_shape=(
            jax.ShapeDtypeStruct((4, 1024), BF16),
            jax.ShapeDtypeStruct((512, 512), F32),
        ),
        in_specs=[vmem] * 5,
        out_specs=(vmem, vmem),
        scratch_shapes=[
            pltpu.VMEM((512, 512), BF16),
            pltpu.VMEM((256, MSG), F32),
            pltpu.VMEM((256, MSG), F32),
            pltpu.VMEM((16, MSG), F32),
            pltpu.VMEM((16, MSG), F32),
            pltpu.VMEM((4096, 512), BF16),
            pltpu.VMEM((256, 1024), BF16),
            pltpu.SemaphoreType.DMA,
            pltpu.SemaphoreType.DMA,
            pltpu.SemaphoreType.DMA,
            pltpu.SemaphoreType.DMA,
            pltpu.SemaphoreType.DMA,
            pltpu.SemaphoreType.DMA((8,)),
            pltpu.SemaphoreType.DMA((9, 8)),
        ],
        compiler_params=pltpu.CompilerParams(
            collective_id=0, has_side_effects=True, vmem_limit_bytes=48 * 1024 * 1024
        ),
    )(embeddings, assign.reshape(1, -1), cluster_list, owner_map, old_centroids)


def solution(mesh):
    rows = P(("group", "member"), None)
    return jax.shard_map(
        shards,
        mesh=mesh,
        in_specs=(rows, P(("group", "member")), rows, P("group", None), rows),
        out_specs=(rows, rows),
        check_vma=False,
    )
```

```python
import math

import jax
import jax.numpy as jnp
from jax import lax
from jax.experimental import pallas as pl
from jax.experimental.pallas import tpu as pltpu
from jax.sharding import PartitionSpec as P

F32, BF16, I32 = jnp.float32, jnp.bfloat16, jnp.int32
MSG = 640
OFFSETS = (0, 1, -1, 2, -2, 3, -3, 4)
BATCHES = ((0, 1), (1, 3), (3, 5), (5, 7), (7, 8))


def iota(shape, dim):
    return lax.broadcasted_iota(I32, shape, dim)


def split3(v):
    hi = v.astype(BF16)
    rest = v - hi.astype(F32)
    mid = rest.astype(BF16)
    low = (rest - mid.astype(F32)).astype(BF16)
    return hi, mid, low


def column_of(row, n):
    eye = iota((n, n), 0) == iota((n, n), 1)
    return jnp.sum(jnp.where(eye, row, 0), axis=1, keepdims=True)


def row_of(col, n):
    eye = iota((n, n), 0) == iota((n, n), 1)
    return jnp.sum(jnp.where(eye, col, 0), axis=0, keepdims=True)


def slot_rows(list_row, pos_row):
    lists = list_row.shape[1]
    listed = jnp.max(
        jnp.where(list_row == iota((256, lists), 0), 1, 0), axis=1, keepdims=True
    )
    pos_col = column_of(pos_row, 256)
    key = jnp.where(listed > 0, pos_col, -8)
    rank = jnp.sum(
        jnp.where(((key >> 2) == (pos_row >> 2)) & (key < pos_row), 1, 0), axis=0, keepdims=True
    )
    listed_row = row_of(listed, 256)
    chip = pos_row >> 4
    core = (pos_row >> 2) & 1
    high = (pos_row >> 3) & 1
    turned = ((chip & 3) << 2) | (chip >> 2)
    target = core * 16 + jnp.where(core == 0, chip, turned)
    slot = jnp.where(listed_row > 0, target * 4 + high * 2 + rank + 1, 0)
    return slot, high * 4 + (pos_row & 3)


def kernel(
    emb_hbm, assign_hbm, listing_hbm, owner_hbm, old_hbm, cent_out, out,
    emb, assign, listing, owner, old,
    perm, send, recv, zsend, zrecv, raw, slab,
    load_sem, a2a_send, a2a_recv, zx_send, zx_recv, ag_send, z_recv, a_recv, b_recv, core_recv,
):
    g = lax.axis_index("group")
    m = lax.axis_index("member")
    x, y, zh, c = m // 16, (m // 4) % 4, (m // 2) % 2, m % 2
    z = zh * 8 + g
    a = jnp.where(c == 0, y, x)
    b = jnp.where(c == 0, x, y)
    me = c * 16 + b * 4 + a

    def at_plane(core, bb, aa):
        xx = jnp.where(core == 0, bb, aa)
        yy = jnp.where(core == 0, aa, bb)
        return {"member": xx * 16 + yy * 4 + zh * 2 + core}

    def at_z(zz):
        zz = (zz + 16) % 16
        return {"group": zz % 8, "member": x * 16 + y * 4 + (zz // 8) * 2 + c}

    def plane_peer(i):
        t = (me + i) % 32
        return t, at_plane(t // 16, (t // 4) % 4, t % 4)

    barrier = pltpu.get_barrier_semaphore()

    def greet(i, carry):
        pl.semaphore_signal(barrier, inc=1, device_id=plane_peer(i)[1])
        return carry

    lax.fori_loop(1, 32, greet, 0)
    for d in (1, -1, 2, -2, 3, -3, 4, -4):
        pl.semaphore_signal(barrier, inc=1, device_id=at_z(z + d))

    loads = [
        pltpu.make_async_copy(src, dst, load_sem.at[i])
        for i, (src, dst) in enumerate(
            ((owner_hbm, owner), (listing_hbm, listing), (assign_hbm, assign), (emb_hbm, emb), (old_hbm, old))
        )
    ]
    for load in loads:
        load.start()
    loads[0].wait()
    loads[1].wait()

    slot_row, line_row = slot_rows(listing[...], owner[...])
    slot_col = column_of(slot_row, 256)
    loads[2].wait()
    row_slot = jnp.sum(
        jnp.where(assign[...] == iota((256, 512), 0), slot_col, 0), axis=0, keepdims=True
    )
    index = iota((256, 1), 0)
    half = (index >> 2) & 1
    wanted = ((index >> 3) << 2 | (index & 3)) + 1
    member_of = row_slot == wanted
    member_f = jnp.where(member_of, 1.0, 0.0)
    count = jnp.sum(member_f, axis=1, keepdims=True)
    member_b = member_f.astype(BF16)
    line = jnp.sum(jnp.where(slot_row == wanted, line_row + 1, 0), axis=1, keepdims=True) - 1
    lane = iota((256, 128), 1)
    mark = jnp.where(((lane & 7) == line) & ((lane >> 3) == half), 1.0, 0.0)
    send[:, 512:] = jnp.where(lane < 16, mark, count)
    loads[3].wait()
    for col in range(0, 512, 256):
        low = jnp.dot(member_b, emb[:, col:col + 256], preferred_element_type=F32)
        high = jnp.dot(member_b, emb[:, 512 + col:512 + col + 256], preferred_element_type=F32)
        send[:, col:col + 256] = jnp.where(half == 0, low, high)

    pl.semaphore_wait(barrier, 39)

    def give(i, carry):
        t, peer = plane_peer(i)
        pltpu.make_async_remote_copy(
            src_ref=send.at[pl.ds(pl.multiple_of(t * 8, 8), 8)],
            dst_ref=recv.at[pl.ds(pl.multiple_of(me * 8, 8), 8)],
            send_sem=a2a_send,
            recv_sem=a2a_recv,
            device_id=peer,
        ).start()
        return carry

    lax.fori_loop(1, 32, give, 0)
    mine = pl.ds(pl.multiple_of(me * 8, 8), 8)
    recv[mine, :] = send[mine, :]

    k = iota((1, 512), 1)
    kc, kb, ka = k >> 8, (k >> 6) & 3, (k >> 4) & 3
    block = jnp.where(kc == 0, kb * 4 + ka, ka * 4 + kb) * 4 + ((k >> 2) & 1) * 2 + kc
    goal = ((k >> 3) & 1) * 256 + (k & 3) * 64 + block
    perm[...] = jnp.where(goal == iota((512, 512), 0), 1.0, 0.0).astype(BF16)
    out[...] = jnp.zeros_like(out)

    def all_but_one(src, dst, ssem, rsem, peer):
        return pltpu.make_async_remote_copy(
            src_ref=src.at[pl.ds(0, 248)], dst_ref=dst.at[pl.ds(0, 248)],
            send_sem=ssem, recv_sem=rsem, device_id=peer,
        )

    whole = all_but_one(send, recv, a2a_send, a2a_recv, plane_peer(1)[1])
    whole.wait_recv()
    marks = jnp.where(lane < 16, recv[:, 512:], 0.0).astype(BF16)
    total = None
    for part in split3(recv[...]):
        term = lax.dot_general(
            marks, part, (((0,), (0,)), ((), ())), preferred_element_type=F32
        )[:16]
        total = term if total is None else total + term
    loads[4].wait()
    line16 = iota((16, 1), 0) & 7
    prior = jnp.zeros((16, 512), F32)
    upper = iota((16, 1), 0) >= 8
    for j in range(4):
        rows = jnp.where(upper, old[j:j + 1, 512:], old[j:j + 1, :512])
        prior = prior + jnp.where(line16 == zh * 4 + j, rows, 0.0)
    zsend[:, :512] = total[:, :512] + prior
    zsend[:, 512:] = total[:, 512:]
    across = [
        pltpu.make_async_remote_copy(
            src_ref=zsend, dst_ref=zrecv.at[i], send_sem=zx_send.at[i], recv_sem=zx_recv.at[i],
            device_id=at_z(z + d),
        )
        for i, d in enumerate((4, -4))
    ]
    for move in across:
        move.start()
    for move in across:
        move.wait_recv()
    tally = zrecv[0, :, 512 + 16:512 + 17] + zrecv[1, :, 512 + 16:512 + 17]
    updated = (zrecv[0, :, :512] + zrecv[1, :, :512]) / (tally + 1.0)
    squares = jnp.sum(updated * updated, axis=1, keepdims=True)
    mean = (squares[:8] + squares[8:]) * (1.0 / 1024)
    scale = lax.rsqrt(mean + 1e-05)
    raw[c, 0, b, a] = (updated * jnp.concatenate([scale, scale], axis=0)).astype(BF16)

    def copy(ref, sem, peer):
        return pltpu.make_async_remote_copy(
            src_ref=ref, dst_ref=ref, send_sem=ag_send, recv_sem=sem, device_id=peer
        )

    sibling = {"member": m + 1 - 2 * c}

    def z_piece(n):
        return pltpu.make_async_remote_copy(
            src_ref=raw.at[c, 0, b, a], dst_ref=raw.at[c, n, b, a],
            send_sem=ag_send, recv_sem=z_recv.at[n], device_id=at_z(z - OFFSETS[n]),
        )

    for n in range(1, 8):
        z_piece(n).start()

    def along_a(k, i, back):
        lo, hi = BATCHES[k]
        aa = (a + 4 - i) % 4 if back else a
        return copy(raw.at[c, lo:hi, b, aa], a_recv.at[k, i], at_plane(c, b, (a + i) % 4))

    def along_b(k, i, back):
        lo, hi = BATCHES[k]
        bb = (b + 4 - i) % 4 if back else b
        return copy(raw.at[c, lo:hi, bb], b_recv.at[k, i], at_plane(c, (b + i) % 4, a))

    def across_cores(k, core):
        lo, hi = BATCHES[k]
        return copy(raw.at[core, lo:hi], core_recv.at[k], sibling)

    def stage_z(k):
        for n in range(*BATCHES[k]):
            if n:
                z_piece(n).wait_recv()
        for i in (1, 3, 2):
            along_a(k, i, False).start()

    def stage_a(k):
        for i in (1, 3, 2):
            along_a(k, i, True).wait_recv()
        for i in (1, 3, 2):
            along_b(k, i, False).start()

    def stage_b(k):
        for i in (1, 3, 2):
            along_b(k, i, True).wait_recv()
        across_cores(k, c).start()

    def one_group(n, carry):
        offset = jnp.where(n % 2 == 1, (n + 1) // 2, -(n // 2))
        gg = (z + offset + 20) % 8
        first = raw[0, n].reshape(256, 512)
        second = raw[1, n].reshape(256, 512)
        for h in range(2):
            rows = slice(256 * h, 256 * h + 256)
            turned = jnp.dot(perm[rows, :256], first, preferred_element_type=F32)
            turned = turned + jnp.dot(perm[rows, 256:], second, preferred_element_type=F32)
            slab[:, 512 * h:512 * h + 512] = turned.astype(BF16)
        lanes = pl.ds(pl.multiple_of((gg // 2) * 128, 128), 128)
        for r in range(0, 512, 256):
            sim = lax.dot_general(
                emb[r:r + 256, :], slab[...], (((1,), (1,)), ((), ())), preferred_element_type=F32
            )
            best = jnp.maximum(sim[:, :128], sim[:, 128:])
            best = jnp.maximum(best, pltpu.roll(best, 64, 1)) * (1.0 / math.sqrt(1024))
            keep = (iota((256, 128), 1) >> 6) == gg % 2
            out[r:r + 256, lanes] = jnp.where(keep, best, out[r:r + 256, lanes])
        return carry

    def stage_dot(k):
        across_cores(k, 1 - c).wait_recv()
        lax.fori_loop(*BATCHES[k], one_group, 0)

    stage_z(0)
    stage_z(1)
    stage_z(2)
    stage_a(0)
    stage_z(3)
    stage_z(4)
    own = raw[c, 7, b, a].astype(F32)
    for h in range(2):
        part = own[8 * h:8 * h + 8]
        cent_out[:, 512 * h:512 * h + 512] = jnp.where(zh == 0, part[:4], part[4:]).astype(BF16)
    stage_a(1)
    stage_a(2)
    stage_b(0)
    stage_a(3)
    stage_a(4)
    stage_dot(0)
    stage_b(1)
    stage_b(2)
    stage_dot(1)
    stage_b(3)
    stage_dot(2)
    stage_b(4)
    stage_dot(3)
    stage_dot(4)

    whole.wait_send()
    for move in across:
        move.wait_send()
    sent = raw.reshape(4096, 512).at[pl.ds(0, 255 * 16)]
    copy(sent, z_recv.at[0], sibling).wait_send()


def shards(embeddings, assign, cluster_list, owner_map, old_centroids):
    vmem = pl.BlockSpec(memory_space=pltpu.VMEM)
    return pl.pallas_call(
        kernel,
        out_shape=(
            jax.ShapeDtypeStruct((4, 1024), BF16),
            jax.ShapeDtypeStruct((512, 512), F32),
        ),
        in_specs=[pl.BlockSpec(memory_space=pl.ANY)] * 5,
        out_specs=(vmem, vmem),
        scratch_shapes=[
            pltpu.VMEM((512, 1024), BF16),
            pltpu.VMEM((1, 512), I32),
            pltpu.VMEM((1, 64), I32),
            pltpu.VMEM((1, 256), I32),
            pltpu.VMEM((4, 1024), F32),
            pltpu.VMEM((512, 512), BF16),
            pltpu.VMEM((256, MSG), F32),
            pltpu.VMEM((256, MSG), F32),
            pltpu.VMEM((16, MSG), F32),
            pltpu.VMEM((2, 16, MSG), F32),
            pltpu.VMEM((2, 8, 4, 4, 16, 512), BF16),
            pltpu.VMEM((256, 1024), BF16),
            pltpu.SemaphoreType.DMA((5,)),
            pltpu.SemaphoreType.DMA,
            pltpu.SemaphoreType.DMA,
            pltpu.SemaphoreType.DMA((2,)),
            pltpu.SemaphoreType.DMA((2,)),
            pltpu.SemaphoreType.DMA,
            pltpu.SemaphoreType.DMA((8,)),
            pltpu.SemaphoreType.DMA((5, 4)),
            pltpu.SemaphoreType.DMA((5, 4)),
            pltpu.SemaphoreType.DMA((5,)),
        ],
        compiler_params=pltpu.CompilerParams(
            collective_id=0, has_side_effects=True, vmem_limit_bytes=60 * 1024 * 1024
        ),
    )(embeddings, assign.reshape(1, -1), cluster_list, owner_map, old_centroids)


def solution(mesh):
    rows = P(("group", "member"), None)
    return jax.shard_map(
        shards,
        mesh=mesh,
        in_specs=(rows, P(("group", "member")), rows, P("group", None), rows),
        out_specs=(rows, rows),
        check_vma=False,
    )
```

```python
import math

import jax
import jax.numpy as jnp
from jax import lax
from jax.experimental import pallas as pl
from jax.experimental.pallas import tpu as pltpu
from jax.sharding import PartitionSpec as P

F32, BF16, I32, I16 = jnp.float32, jnp.bfloat16, jnp.int32, jnp.int16
MSG = 384
ZMSG = 640
OFFSETS = (0, 1, -1, 2, -2, 3, -3, 4)
BATCHES = ((0, 1), (1, 3), (3, 5), (5, 7), (7, 8))


def iota(shape, dim):
    return lax.broadcasted_iota(I32, shape, dim)


def split2(v):
    high = v.astype(BF16)
    return high, (v - high.astype(F32)).astype(BF16)


def quantise(v):
    top = jnp.maximum(jnp.max(jnp.abs(v), axis=1, keepdims=True), 1e-30)
    exponent = jnp.ceil(jnp.log2(top * (1.0 / 32000)))
    return jnp.floor(v * jnp.exp2(-exponent) + 0.5).astype(I32).astype(I16), exponent


def column_of(row, n):
    eye = iota((n, n), 0) == iota((n, n), 1)
    return jnp.sum(jnp.where(eye, row, 0), axis=1, keepdims=True)


def row_of(col, n):
    eye = iota((n, n), 0) == iota((n, n), 1)
    return jnp.sum(jnp.where(eye, col, 0), axis=0, keepdims=True)


def slot_rows(list_row, pos_row):
    lists = list_row.shape[1]
    listed = jnp.max(
        jnp.where(list_row == iota((256, lists), 0), 1, 0), axis=1, keepdims=True
    )
    pos_col = column_of(pos_row, 256)
    key = jnp.where(listed > 0, pos_col, -8)
    rank = jnp.sum(
        jnp.where(((key >> 2) == (pos_row >> 2)) & (key < pos_row), 1, 0), axis=0, keepdims=True
    )
    listed_row = row_of(listed, 256)
    chip = pos_row >> 4
    core = (pos_row >> 2) & 1
    high = (pos_row >> 3) & 1
    turned = ((chip & 3) << 2) | (chip >> 2)
    target = core * 16 + jnp.where(core == 0, chip, turned)
    slot = jnp.where(listed_row > 0, target * 4 + high * 2 + rank + 1, 0)
    return slot, high * 4 + (pos_row & 3)


def kernel(
    emb_hbm, assign_hbm, listing_hbm, owner_hbm, old_hbm, cent_out, out,
    emb, assign, listing, owner, old,
    perm, send, recv, zsend, zrecv, raw, slab,
    load_sem, a2a_send, a2a_recv, zx_send, zx_recv, ag_send, z_recv, a_recv, b_recv, core_recv,
):
    g = lax.axis_index("group")
    m = lax.axis_index("member")
    x, y, zh, c = m // 16, (m // 4) % 4, (m // 2) % 2, m % 2
    z = zh * 8 + g
    a = jnp.where(c == 0, y, x)
    b = jnp.where(c == 0, x, y)
    me = c * 16 + b * 4 + a

    def at_plane(core, bb, aa):
        xx = jnp.where(core == 0, bb, aa)
        yy = jnp.where(core == 0, aa, bb)
        return {"member": xx * 16 + yy * 4 + zh * 2 + core}

    def at_z(zz):
        zz = (zz + 16) % 16
        return {"group": zz % 8, "member": x * 16 + y * 4 + (zz // 8) * 2 + c}

    def plane_peer(i):
        def step(j):
            return jnp.where(j == 0, 2, jnp.where(j == 1, 1, jnp.where(j == 2, 3, 0)))

        xx = (x + step(i // 8)) % 4
        yy = (y + step((i // 2) % 4)) % 4
        core = (c + i + 1) % 2
        t = core * 16 + jnp.where(core == 0, xx * 4 + yy, yy * 4 + xx)
        return t, {"member": xx * 16 + yy * 4 + zh * 2 + core}

    barrier = pltpu.get_barrier_semaphore()

    def greet(i, carry):
        pl.semaphore_signal(barrier, inc=1, device_id=plane_peer(i)[1])
        return carry

    lax.fori_loop(0, 31, greet, 0)
    for d in (1, -1, 2, -2, 3, -3, 4, -4):
        pl.semaphore_signal(barrier, inc=1, device_id=at_z(z + d))

    loads = [
        pltpu.make_async_copy(src, dst, load_sem.at[i])
        for i, (src, dst) in enumerate(
            ((owner_hbm, owner), (listing_hbm, listing), (assign_hbm, assign), (emb_hbm, emb), (old_hbm, old))
        )
    ]
    for load in loads:
        load.start()
    loads[0].wait()
    loads[1].wait()

    slot_row, line_row = slot_rows(listing[...], owner[...])
    slot_col = column_of(slot_row, 256)
    loads[2].wait()
    row_slot = jnp.sum(
        jnp.where(assign[...] == iota((256, 512), 0), slot_col, 0), axis=0, keepdims=True
    )
    index = iota((512, 1), 0)
    quarter = (index >> 2) & 3
    wanted = ((index >> 4) << 2 | (index & 3)) + 1
    member_f = jnp.where(row_slot == wanted, 1.0, 0.0)
    count = jnp.sum(member_f, axis=1, keepdims=True)
    member_b = member_f.astype(BF16)
    line = jnp.sum(jnp.where(slot_row == wanted, line_row + 1, 0), axis=1, keepdims=True) - 1
    lane = iota((512, 128), 1)
    mark = jnp.where(((lane & 7) == line) & ((lane >> 3) == quarter), 1.0, 0.0)
    loads[3].wait()
    partial = jnp.zeros((512, 256), F32)
    for k in range(4):
        term = jnp.dot(member_b, emb[:, 256 * k:256 * k + 256], preferred_element_type=F32)
        partial = jnp.where(quarter == k, term, partial)
    send[:, :256], exponent = quantise(partial)
    notes = jnp.where(lane < 32, mark, jnp.where(lane < 64, count, exponent))
    send[:, 256:] = notes.astype(I32).astype(I16)

    pl.semaphore_wait(barrier, 39)

    def give(i, carry):
        t, peer = plane_peer(i)
        pltpu.make_async_remote_copy(
            src_ref=send.at[pl.ds(pl.multiple_of(t * 16, 16), 16)],
            dst_ref=recv.at[pl.ds(pl.multiple_of(me * 16, 16), 16)],
            send_sem=a2a_send,
            recv_sem=a2a_recv,
            device_id=peer,
        ).start()
        return carry

    lax.fori_loop(0, 31, give, 0)
    mine = pl.ds(pl.multiple_of(me * 16, 16), 16)
    recv[mine, :] = send[mine, :]

    k = iota((1, 512), 1)
    kc, kb, ka = k >> 8, (k >> 6) & 3, (k >> 4) & 3
    block = jnp.where(kc == 0, kb * 4 + ka, ka * 4 + kb) * 4 + ((k >> 2) & 1) * 2 + kc
    goal = ((k >> 3) & 1) * 256 + (k & 3) * 64 + block
    perm[...] = jnp.where(goal == iota((512, 512), 0), 1.0, 0.0).astype(BF16)
    out[...] = jnp.zeros_like(out)

    def all_but_one(src, dst, ssem, rsem, peer):
        return pltpu.make_async_remote_copy(
            src_ref=src.at[pl.ds(0, 496)], dst_ref=dst.at[pl.ds(0, 496)],
            send_sem=ssem, recv_sem=rsem, device_id=peer,
        )

    whole = all_but_one(send, recv, a2a_send, a2a_recv, plane_peer(0)[1])
    whole.wait_recv()
    notes = recv[:, 256:].astype(I32).astype(F32)
    marks = jnp.where(lane < 32, notes, 0.0)
    scaled = (marks * jnp.exp2(notes[:, 64:65])).astype(BF16)
    marks = marks.astype(BF16)

    def gathered(weights, values):
        return lax.dot_general(
            weights, values, (((0,), (0,)), ((), ())), preferred_element_type=F32
        )[:32]

    high, low = split2(recv[:, :256].astype(I32).astype(F32))
    total = gathered(scaled, high) + gathered(scaled, low)
    high, low = split2(notes)
    tally = (gathered(marks, high) + gathered(marks, low))[:16, 32:33]
    loads[4].wait()
    line8 = iota((8, 1), 0)
    parts = []
    for k in range(4):
        part = total[8 * k:8 * k + 8]
        for j in range(4):
            part = part + jnp.where(line8 == zh * 4 + j, old[j:j + 1, 256 * k:256 * k + 256], 0.0)
        parts.append(part)
    sums = jnp.concatenate(
        [jnp.concatenate(parts[:2], axis=1), jnp.concatenate(parts[2:], axis=1)], axis=0
    )
    zsend[:, :512], exponent = quantise(sums)
    notes = jnp.where(iota((16, 128), 1) < 64, tally, exponent)
    zsend[:, 512:] = notes.astype(I32).astype(I16)

    across = [
        pltpu.make_async_remote_copy(
            src_ref=zsend, dst_ref=zrecv.at[i], send_sem=zx_send.at[i], recv_sem=zx_recv.at[i],
            device_id=at_z(z + d),
        )
        for i, d in enumerate((4, -4))
    ]
    for move in across:
        move.start()
    for move in across:
        move.wait_recv()
    sums = jnp.zeros((16, 512), F32)
    tally = jnp.zeros((16, 1), F32)
    for i in range(2):
        notes = zrecv[i, :, 512:].astype(I32).astype(F32)
        sums = sums + zrecv[i, :, :512].astype(I32).astype(F32) * jnp.exp2(notes[:, 64:65])
        tally = tally + notes[:, :1]
    updated = sums / (tally + 1.0)
    squares = jnp.sum(updated * updated, axis=1, keepdims=True)
    mean = (squares[:8] + squares[8:]) * (1.0 / 1024)
    scale = lax.rsqrt(mean + 1e-05)
    raw[c, 0, b, a] = (updated * jnp.concatenate([scale, scale], axis=0)).astype(BF16)

    def copy(ref, sem, peer):
        return pltpu.make_async_remote_copy(
            src_ref=ref, dst_ref=ref, send_sem=ag_send, recv_sem=sem, device_id=peer
        )

    sibling = {"member": m + 1 - 2 * c}

    def z_piece(n):
        return pltpu.make_async_remote_copy(
            src_ref=raw.at[c, 0, b, a], dst_ref=raw.at[c, n, b, a],
            send_sem=ag_send, recv_sem=z_recv.at[n], device_id=at_z(z - OFFSETS[n]),
        )

    for n in (7, 5, 6, 3, 4, 1, 2):
        z_piece(n).start()

    def along_a(k, i, back):
        lo, hi = BATCHES[k]
        aa = (a + 4 - i) % 4 if back else a
        return copy(raw.at[c, lo:hi, b, aa], a_recv.at[k, i], at_plane(c, b, (a + i) % 4))

    def along_b(k, i, back):
        lo, hi = BATCHES[k]
        bb = (b + 4 - i) % 4 if back else b
        return copy(raw.at[c, lo:hi, bb], b_recv.at[k, i], at_plane(c, (b + i) % 4, a))

    def across_cores(k, core):
        lo, hi = BATCHES[k]
        return copy(raw.at[core, lo:hi], core_recv.at[k], sibling)

    def stage_z(k):
        for n in range(*BATCHES[k]):
            if n:
                z_piece(n).wait_recv()
        for i in (2, 1, 3):
            along_a(k, i, False).start()

    def stage_a(k):
        for i in (1, 3, 2):
            along_a(k, i, True).wait_recv()
        for i in (2, 1, 3):
            along_b(k, i, False).start()

    def stage_b(k):
        for i in (1, 3, 2):
            along_b(k, i, True).wait_recv()
        across_cores(k, c).start()

    def one_group(n, carry):
        offset = jnp.where(n % 2 == 1, (n + 1) // 2, -(n // 2))
        gg = (z + offset + 20) % 8
        first = raw[0, n].reshape(256, 512)
        second = raw[1, n].reshape(256, 512)
        for h in range(2):
            rows = slice(256 * h, 256 * h + 256)
            turned = jnp.dot(perm[rows, :256], first, preferred_element_type=F32)
            turned = turned + jnp.dot(perm[rows, 256:], second, preferred_element_type=F32)
            slab[:, 512 * h:512 * h + 512] = turned.astype(BF16)
        lanes = pl.ds(pl.multiple_of((gg // 2) * 128, 128), 128)
        for r in range(0, 512, 256):
            sim = lax.dot_general(
                emb[r:r + 256, :], slab[...], (((1,), (1,)), ((), ())), preferred_element_type=F32
            )
            best = jnp.maximum(sim[:, :128], sim[:, 128:])
            best = jnp.maximum(best, pltpu.roll(best, 64, 1)) * (1.0 / math.sqrt(1024))
            keep = (iota((256, 128), 1) >> 6) == gg % 2
            out[r:r + 256, lanes] = jnp.where(keep, best, out[r:r + 256, lanes])
        return carry

    def stage_dot(k):
        across_cores(k, 1 - c).wait_recv()
        lax.fori_loop(*BATCHES[k], one_group, 0)

    stage_z(0)
    stage_z(1)
    stage_z(2)
    stage_a(0)
    stage_z(3)
    stage_z(4)
    own = raw[c, 7, b, a].astype(F32)
    for h in range(2):
        part = own[8 * h:8 * h + 8]
        cent_out[:, 512 * h:512 * h + 512] = jnp.where(zh == 0, part[:4], part[4:]).astype(BF16)
    stage_a(1)
    stage_a(2)
    stage_b(0)
    stage_a(3)
    stage_a(4)
    stage_dot(0)
    stage_b(1)
    stage_b(2)
    stage_dot(1)
    stage_b(3)
    stage_dot(2)
    stage_b(4)
    stage_dot(3)
    stage_dot(4)

    whole.wait_send()
    for move in across:
        move.wait_send()
    sent = raw.reshape(4096, 512).at[pl.ds(0, 255 * 16)]
    copy(sent, z_recv.at[0], sibling).wait_send()


def shards(embeddings, assign, cluster_list, owner_map, old_centroids):
    vmem = pl.BlockSpec(memory_space=pltpu.VMEM)
    return pl.pallas_call(
        kernel,
        out_shape=(
            pltpu.VMEM((4, 1024), BF16),
            pltpu.VMEM((512, 512), F32),
        ),
        in_specs=[pl.BlockSpec(memory_space=pl.ANY)] * 5,
        out_specs=(vmem, vmem),
        scratch_shapes=[
            pltpu.VMEM((512, 1024), BF16),
            pltpu.VMEM((1, 512), I32),
            pltpu.VMEM((1, 64), I32),
            pltpu.VMEM((1, 256), I32),
            pltpu.VMEM((4, 1024), F32),
            pltpu.VMEM((512, 512), BF16),
            pltpu.VMEM((512, MSG), I16),
            pltpu.VMEM((512, MSG), I16),
            pltpu.VMEM((16, ZMSG), I16),
            pltpu.VMEM((2, 16, ZMSG), I16),
            pltpu.VMEM((2, 8, 4, 4, 16, 512), BF16),
            pltpu.VMEM((256, 1024), BF16),
            pltpu.SemaphoreType.DMA((5,)),
            pltpu.SemaphoreType.DMA,
            pltpu.SemaphoreType.DMA,
            pltpu.SemaphoreType.DMA((2,)),
            pltpu.SemaphoreType.DMA((2,)),
            pltpu.SemaphoreType.DMA,
            pltpu.SemaphoreType.DMA((8,)),
            pltpu.SemaphoreType.DMA((5, 4)),
            pltpu.SemaphoreType.DMA((5, 4)),
            pltpu.SemaphoreType.DMA((5,)),
        ],
        compiler_params=pltpu.CompilerParams(
            collective_id=0, has_side_effects=True, vmem_limit_bytes=60 * 1024 * 1024
        ),
    )(embeddings, assign.reshape(1, -1), cluster_list, owner_map, old_centroids)


def solution(mesh):
    rows = P(("group", "member"), None)
    return jax.shard_map(
        shards,
        mesh=mesh,
        in_specs=(rows, P(("group", "member")), rows, P("group", None), rows),
        out_specs=(rows, rows),
        check_vma=False,
    )
```

```python
import math

import jax
import jax.numpy as jnp
from jax import lax
from jax.experimental import pallas as pl
from jax.experimental.pallas import tpu as pltpu
from jax.sharding import PartitionSpec as P

F32, BF16, I32, I16 = jnp.float32, jnp.bfloat16, jnp.int32, jnp.int16
MSG = 384
ZMSG = 640
OFFSETS = (0, 1, -1, 2, -2, 3, -3, 4)
SIDE = {1: (0, -1, 3), 2: (0, 1, 1), 5: (3, -1, 3), 6: (4, 1, 1)}
BATCHES = ((0, 1), (1, 3), (3, 5), (5, 7), (7, 8))


def iota(shape, dim):
    return lax.broadcasted_iota(I32, shape, dim)


def split2(v):
    high = v.astype(BF16)
    return high, (v - high.astype(F32)).astype(BF16)


def quantise(v):
    top = jnp.maximum(jnp.max(jnp.abs(v), axis=1, keepdims=True), 1e-30)
    exponent = jnp.ceil(jnp.log2(top * (1.0 / 32000)))
    return jnp.floor(v * jnp.exp2(-exponent) + 0.5).astype(I32).astype(I16), exponent


def column_of(row, n):
    eye = iota((n, n), 0) == iota((n, n), 1)
    return jnp.sum(jnp.where(eye, row, 0), axis=1, keepdims=True)


def row_of(col, n):
    eye = iota((n, n), 0) == iota((n, n), 1)
    return jnp.sum(jnp.where(eye, col, 0), axis=0, keepdims=True)


def slot_rows(list_row, pos_row):
    lists = list_row.shape[1]
    listed = jnp.max(
        jnp.where(list_row == iota((256, lists), 0), 1, 0), axis=1, keepdims=True
    )
    pos_col = column_of(pos_row, 256)
    key = jnp.where(listed > 0, pos_col, -8)
    rank = jnp.sum(
        jnp.where(((key >> 2) == (pos_row >> 2)) & (key < pos_row), 1, 0), axis=0, keepdims=True
    )
    listed_row = row_of(listed, 256)
    chip = pos_row >> 4
    core = (pos_row >> 2) & 1
    high = (pos_row >> 3) & 1
    turned = ((chip & 3) << 2) | (chip >> 2)
    target = core * 16 + jnp.where(core == 0, chip, turned)
    slot = jnp.where(listed_row > 0, target * 4 + high * 2 + rank + 1, 0)
    return slot, high * 4 + (pos_row & 3)


def kernel(
    emb_hbm, assign_hbm, listing_hbm, owner_hbm, old_hbm, cent_out, out,
    emb, assign, listing, owner, old,
    perm, send, recv, zsend, zrecv, raw, slab,
    load_sem, a2a_send, a2a_recv, zx_send, zx_recv, ag_send, z_recv, a_recv, b_recv, side_recv, core_recv,
):
    g = lax.axis_index("group")
    m = lax.axis_index("member")
    x, y, zh, c = m // 16, (m // 4) % 4, (m // 2) % 2, m % 2
    z = zh * 8 + g
    a = jnp.where(c == 0, y, x)
    b = jnp.where(c == 0, x, y)
    me = c * 16 + b * 4 + a

    def at_plane(core, bb, aa):
        xx = jnp.where(core == 0, bb, aa)
        yy = jnp.where(core == 0, aa, bb)
        return {"member": xx * 16 + yy * 4 + zh * 2 + core}

    def at_z(zz):
        zz = (zz + 16) % 16
        return {"group": zz % 8, "member": x * 16 + y * 4 + (zz // 8) * 2 + c}

    def plane_peer(i):
        def step(j):
            return jnp.where(j == 0, 2, jnp.where(j == 1, 1, jnp.where(j == 2, 3, 0)))

        xx = (x + step(i // 8)) % 4
        yy = (y + step((i // 2) % 4)) % 4
        core = (c + i + 1) % 2
        t = core * 16 + jnp.where(core == 0, xx * 4 + yy, yy * 4 + xx)
        return t, {"member": xx * 16 + yy * 4 + zh * 2 + core}

    barrier = pltpu.get_barrier_semaphore()

    def greet(i, carry):
        pl.semaphore_signal(barrier, inc=1, device_id=plane_peer(i)[1])
        return carry

    lax.fori_loop(0, 31, greet, 0)
    for d in (1, -1, 2, -2, 3, -3, 4, -4):
        pl.semaphore_signal(barrier, inc=1, device_id=at_z(z + d))

    loads = [
        pltpu.make_async_copy(src, dst, load_sem.at[i])
        for i, (src, dst) in enumerate(
            ((owner_hbm, owner), (listing_hbm, listing), (assign_hbm, assign), (emb_hbm, emb), (old_hbm, old))
        )
    ]
    for load in loads:
        load.start()
    loads[0].wait()
    loads[1].wait()

    slot_row, line_row = slot_rows(listing[...], owner[...])
    slot_col = column_of(slot_row, 256)
    loads[2].wait()
    row_slot = jnp.sum(
        jnp.where(assign[...] == iota((256, 512), 0), slot_col, 0), axis=0, keepdims=True
    )
    index = iota((512, 1), 0)
    quarter = (index >> 2) & 3
    wanted = ((index >> 4) << 2 | (index & 3)) + 1
    member_f = jnp.where(row_slot == wanted, 1.0, 0.0)
    count = jnp.sum(member_f, axis=1, keepdims=True)
    member_b = member_f.astype(BF16)
    line = jnp.sum(jnp.where(slot_row == wanted, line_row + 1, 0), axis=1, keepdims=True) - 1
    lane = iota((512, 128), 1)
    mark = jnp.where(((lane & 7) == line) & ((lane >> 3) == quarter), 1.0, 0.0)
    loads[3].wait()
    partial = jnp.zeros((512, 256), F32)
    for k in range(4):
        term = jnp.dot(member_b, emb[:, 256 * k:256 * k + 256], preferred_element_type=F32)
        partial = jnp.where(quarter == k, term, partial)
    send[:, :256], exponent = quantise(partial)
    notes = jnp.where(lane < 32, mark, jnp.where(lane < 64, count, exponent))
    send[:, 256:] = notes.astype(I32).astype(I16)

    pl.semaphore_wait(barrier, 39)

    def give(i, carry):
        t, peer = plane_peer(i)
        pltpu.make_async_remote_copy(
            src_ref=send.at[pl.ds(pl.multiple_of(t * 16, 16), 16)],
            dst_ref=recv.at[pl.ds(pl.multiple_of(me * 16, 16), 16)],
            send_sem=a2a_send,
            recv_sem=a2a_recv,
            device_id=peer,
        ).start()
        return carry

    lax.fori_loop(0, 31, give, 0)
    mine = pl.ds(pl.multiple_of(me * 16, 16), 16)
    recv[mine, :] = send[mine, :]

    k = iota((1, 512), 1)
    kc, kb, ka = k >> 8, (k >> 6) & 3, (k >> 4) & 3
    block = jnp.where(kc == 0, kb * 4 + ka, ka * 4 + kb) * 4 + ((k >> 2) & 1) * 2 + kc
    goal = ((k >> 3) & 1) * 256 + (k & 3) * 64 + block
    perm[...] = jnp.where(goal == iota((512, 512), 0), 1.0, 0.0).astype(BF16)
    out[...] = jnp.zeros_like(out)

    def all_but_one(src, dst, ssem, rsem, peer):
        return pltpu.make_async_remote_copy(
            src_ref=src.at[pl.ds(0, 496)], dst_ref=dst.at[pl.ds(0, 496)],
            send_sem=ssem, recv_sem=rsem, device_id=peer,
        )

    whole = all_but_one(send, recv, a2a_send, a2a_recv, plane_peer(0)[1])
    whole.wait_recv()
    notes = recv[:, 256:].astype(I32).astype(F32)
    marks = jnp.where(lane < 32, notes, 0.0)
    scaled = (marks * jnp.exp2(notes[:, 64:65])).astype(BF16)
    marks = marks.astype(BF16)

    def gathered(weights, values):
        return lax.dot_general(
            weights, values, (((0,), (0,)), ((), ())), preferred_element_type=F32
        )[:32]

    high, low = split2(recv[:, :256].astype(I32).astype(F32))
    total = gathered(scaled, high) + gathered(scaled, low)
    high, low = split2(notes)
    tally = (gathered(marks, high) + gathered(marks, low))[:16, 32:33]
    loads[4].wait()
    line8 = iota((8, 1), 0)
    parts = []
    for k in range(4):
        part = total[8 * k:8 * k + 8]
        for j in range(4):
            part = part + jnp.where(line8 == zh * 4 + j, old[j:j + 1, 256 * k:256 * k + 256], 0.0)
        parts.append(part)
    sums = jnp.concatenate(
        [jnp.concatenate(parts[:2], axis=1), jnp.concatenate(parts[2:], axis=1)], axis=0
    )
    zsend[:, :512], exponent = quantise(sums)
    notes = jnp.where(iota((16, 128), 1) < 64, tally, exponent)
    zsend[:, 512:] = notes.astype(I32).astype(I16)

    across = [
        pltpu.make_async_remote_copy(
            src_ref=zsend, dst_ref=zrecv.at[i], send_sem=zx_send.at[i], recv_sem=zx_recv.at[i],
            device_id=at_z(z + d),
        )
        for i, d in enumerate((4, -4))
    ]
    for move in across:
        move.start()
    for move in across:
        move.wait_recv()
    sums = jnp.zeros((16, 512), F32)
    tally = jnp.zeros((16, 1), F32)
    for i in range(2):
        notes = zrecv[i, :, 512:].astype(I32).astype(F32)
        sums = sums + zrecv[i, :, :512].astype(I32).astype(F32) * jnp.exp2(notes[:, 64:65])
        tally = tally + notes[:, :1]
    updated = sums / (tally + 1.0)
    squares = jnp.sum(updated * updated, axis=1, keepdims=True)
    mean = (squares[:8] + squares[8:]) * (1.0 / 1024)
    scale = lax.rsqrt(mean + 1e-05)
    raw[c, 0, b, a] = (updated * jnp.concatenate([scale, scale], axis=0)).astype(BF16)

    def copy(ref, sem, peer):
        return pltpu.make_async_remote_copy(
            src_ref=ref, dst_ref=ref, send_sem=ag_send, recv_sem=sem, device_id=peer
        )

    sibling = {"member": m + 1 - 2 * c}

    def z_piece(n):
        return pltpu.make_async_remote_copy(
            src_ref=raw.at[c, 0, b, a], dst_ref=raw.at[c, n, b, a],
            send_sem=ag_send, recv_sem=z_recv.at[n], device_id=at_z(z - OFFSETS[n]),
        )

    for n in (1, 2, 3, 4, 5, 6, 7):
        z_piece(n).start()

    def along_a(k, i, back):
        lo, hi = BATCHES[k]
        aa = (a + 4 - i) % 4 if back else a
        return copy(raw.at[c, lo:hi, b, aa], a_recv.at[k, i], at_plane(c, b, (a + i) % 4))

    def along_b(k, i, back):
        lo, hi = BATCHES[k]
        if lo % 4 == 1:
            lo, hi = (lo + 1, hi) if i == 1 else (lo, hi - 1)
        bb = (b + 4 - i) % 4 if back else b
        return copy(raw.at[c, lo:hi, bb], b_recv.at[k, i], at_plane(c, (b + i) % 4, a))

    def from_z(n, j):
        source, dz, near = SIDE[n]
        chunk = (b + (2, near)[j]) % 4
        return pltpu.make_async_remote_copy(
            src_ref=raw.at[c, source, chunk], dst_ref=raw.at[c, n, chunk],
            send_sem=ag_send, recv_sem=side_recv.at[n, j], device_id=at_z(z + dz),
        )

    def across_cores(n, core):
        return copy(raw.at[core, n], core_recv.at[n], sibling)

    def stage_z(k):
        for n in range(*BATCHES[k]):
            if n:
                z_piece(n).wait_recv()
        for i in (2, 1, 3):
            along_a(k, i, False).start()

    def peers_of(k):
        return (1, 3) if BATCHES[k][0] % 4 == 1 else (2, 1, 3)

    def stage_a(k):
        for i in (1, 3, 2):
            along_a(k, i, True).wait_recv()
        for i in peers_of(k):
            along_b(k, i, False).start()

    def stage_b(k):
        for i in reversed(peers_of(k)):
            along_b(k, i, True).wait_recv()
        for n in range(*BATCHES[k]):
            for target in SIDE:
                if SIDE[target][0] == n:
                    from_z(target, 0).start()
                    from_z(target, 1).start()
        for n in range(*BATCHES[k]):
            if n in SIDE:
                from_z(n, 0).wait_recv()
                from_z(n, 1).wait_recv()
            across_cores(n, c).start()

    def one_group(n, carry):
        offset = jnp.where(n % 2 == 1, (n + 1) // 2, -(n // 2))
        gg = (z + offset + 20) % 8
        first = raw[0, n].reshape(256, 512)
        second = raw[1, n].reshape(256, 512)
        for h in range(2):
            rows = slice(256 * h, 256 * h + 256)
            turned = jnp.dot(perm[rows, :256], first, preferred_element_type=F32)
            turned = turned + jnp.dot(perm[rows, 256:], second, preferred_element_type=F32)
            slab[:, 512 * h:512 * h + 512] = turned.astype(BF16)
        lanes = pl.ds(pl.multiple_of((gg // 2) * 128, 128), 128)
        for r in range(0, 512, 256):
            sim = lax.dot_general(
                emb[r:r + 256, :], slab[...], (((1,), (1,)), ((), ())), preferred_element_type=F32
            )
            best = jnp.maximum(sim[:, :128], sim[:, 128:])
            best = jnp.maximum(best, pltpu.roll(best, 64, 1)) * (1.0 / math.sqrt(1024))
            keep = (iota((256, 128), 1) >> 6) == gg % 2
            out[r:r + 256, lanes] = jnp.where(keep, best, out[r:r + 256, lanes])
        return carry

    def stage_dot(k):
        def piece(n, carry):
            across_cores(n, 1 - c).wait_recv()
            return one_group(n, carry)

        lax.fori_loop(*BATCHES[k], piece, 0)

    stage_z(0)
    stage_z(1)
    stage_z(2)
    stage_a(0)
    stage_z(3)
    stage_z(4)
    own = raw[c, 7, b, a].astype(F32)
    for h in range(2):
        part = own[8 * h:8 * h + 8]
        cent_out[:, 512 * h:512 * h + 512] = jnp.where(zh == 0, part[:4], part[4:]).astype(BF16)
    stage_a(1)
    stage_b(0)
    stage_a(2)
    stage_a(3)
    stage_a(4)
    stage_dot(0)
    stage_b(1)
    stage_b(2)
    stage_dot(1)
    stage_b(4)
    stage_dot(2)
    stage_b(3)
    stage_dot(4)
    stage_dot(3)

    whole.wait_send()
    for move in across:
        move.wait_send()
    sent = raw.reshape(4096, 512).at[pl.ds(0, 255 * 16)]
    copy(sent, z_recv.at[0], sibling).wait_send()


def shards(embeddings, assign, cluster_list, owner_map, old_centroids):
    vmem = pl.BlockSpec(memory_space=pltpu.VMEM)
    return pl.pallas_call(
        kernel,
        out_shape=(
            pltpu.VMEM((4, 1024), BF16),
            pltpu.VMEM((512, 512), F32),
        ),
        in_specs=[pl.BlockSpec(memory_space=pl.ANY)] * 5,
        out_specs=(vmem, vmem),
        scratch_shapes=[
            pltpu.VMEM((512, 1024), BF16),
            pltpu.VMEM((1, 512), I32),
            pltpu.VMEM((1, 64), I32),
            pltpu.VMEM((1, 256), I32),
            pltpu.VMEM((4, 1024), F32),
            pltpu.VMEM((512, 512), BF16),
            pltpu.VMEM((512, MSG), I16),
            pltpu.VMEM((512, MSG), I16),
            pltpu.VMEM((16, ZMSG), I16),
            pltpu.VMEM((2, 16, ZMSG), I16),
            pltpu.VMEM((2, 8, 4, 4, 16, 512), BF16),
            pltpu.VMEM((256, 1024), BF16),
            pltpu.SemaphoreType.DMA((5,)),
            pltpu.SemaphoreType.DMA,
            pltpu.SemaphoreType.DMA,
            pltpu.SemaphoreType.DMA((2,)),
            pltpu.SemaphoreType.DMA((2,)),
            pltpu.SemaphoreType.DMA,
            pltpu.SemaphoreType.DMA((8,)),
            pltpu.SemaphoreType.DMA((5, 4)),
            pltpu.SemaphoreType.DMA((5, 4)),
            pltpu.SemaphoreType.DMA((8, 2)),
            pltpu.SemaphoreType.DMA((8,)),
        ],
        compiler_params=pltpu.CompilerParams(
            collective_id=0, has_side_effects=True, vmem_limit_bytes=60 * 1024 * 1024
        ),
    )(embeddings, assign.reshape(1, -1), cluster_list, owner_map, old_centroids)


def solution(mesh):
    rows = P(("group", "member"), None)
    return jax.shard_map(
        shards,
        mesh=mesh,
        in_specs=(rows, P(("group", "member")), rows, P("group", None), rows),
        out_specs=(rows, rows),
        check_vma=False,
    )
```

```python
import math

import jax
import jax.numpy as jnp
from jax import lax
from jax.experimental import pallas as pl
from jax.experimental.pallas import tpu as pltpu
from jax.sharding import PartitionSpec as P

F32, BF16, I32, I16 = jnp.float32, jnp.bfloat16, jnp.int32, jnp.int16
MSG = 384
ZMSG = 640
OFFSETS = (0, 1, -1, 2, -2, 3, -3, 4)
SIDE = {1: (0, -1, 3), 2: (0, 1, 1)}
BATCHES = ((0, 1), (1, 3), (3, 5), (5, 7), (7, 8))


def iota(shape, dim):
    return lax.broadcasted_iota(I32, shape, dim)


def split2(v):
    high = v.astype(BF16)
    return high, (v - high.astype(F32)).astype(BF16)


def quantise(v):
    top = jnp.maximum(jnp.max(jnp.abs(v), axis=1, keepdims=True), 1e-30)
    exponent = jnp.ceil(jnp.log2(top * (1.0 / 32000)))
    return jnp.floor(v * jnp.exp2(-exponent) + 0.5).astype(I32).astype(I16), exponent


def column_of(row, n):
    eye = iota((n, n), 0) == iota((n, n), 1)
    return jnp.sum(jnp.where(eye, row, 0), axis=1, keepdims=True)


def row_of(col, n):
    eye = iota((n, n), 0) == iota((n, n), 1)
    return jnp.sum(jnp.where(eye, col, 0), axis=0, keepdims=True)


def slot_rows(list_row, pos_row):
    lists = list_row.shape[1]
    listed = jnp.max(
        jnp.where(list_row == iota((256, lists), 0), 1, 0), axis=1, keepdims=True
    )
    pos_col = column_of(pos_row, 256)
    key = jnp.where(listed > 0, pos_col, -8)
    rank = jnp.sum(
        jnp.where(((key >> 2) == (pos_row >> 2)) & (key < pos_row), 1, 0), axis=0, keepdims=True
    )
    listed_row = row_of(listed, 256)
    chip = pos_row >> 4
    core = (pos_row >> 2) & 1
    high = (pos_row >> 3) & 1
    turned = ((chip & 3) << 2) | (chip >> 2)
    target = core * 16 + jnp.where(core == 0, chip, turned)
    slot = jnp.where(listed_row > 0, target * 4 + high * 2 + rank + 1, 0)
    return slot, high * 4 + (pos_row & 3)


def kernel(
    emb_hbm, assign_hbm, listing_hbm, owner_hbm, old_hbm, cent_out, out,
    emb, assign, listing, owner, old,
    perm, send, recv, zsend, zrecv, raw, slab,
    load_sem, a2a_send, a2a_recv, zx_send, zx_recv, ag_send, z_recv, a_recv, b_recv, side_recv, core_recv,
):
    g = lax.axis_index("group")
    m = lax.axis_index("member")
    x, y, zh, c = m // 16, (m // 4) % 4, (m // 2) % 2, m % 2
    z = zh * 8 + g
    a = jnp.where(c == 0, y, x)
    b = jnp.where(c == 0, x, y)
    me = c * 16 + b * 4 + a

    def at_plane(core, bb, aa):
        xx = jnp.where(core == 0, bb, aa)
        yy = jnp.where(core == 0, aa, bb)
        return {"member": xx * 16 + yy * 4 + zh * 2 + core}

    def at_z(zz):
        zz = (zz + 16) % 16
        return {"group": zz % 8, "member": x * 16 + y * 4 + (zz // 8) * 2 + c}

    def plane_peer(i):
        def step(j):
            return jnp.where(j == 0, 2, jnp.where(j == 1, 1, jnp.where(j == 2, 3, 0)))

        xx = (x + step(i // 8)) % 4
        yy = (y + step((i // 2) % 4)) % 4
        core = (c + i + 1) % 2
        t = core * 16 + jnp.where(core == 0, xx * 4 + yy, yy * 4 + xx)
        return t, {"member": xx * 16 + yy * 4 + zh * 2 + core}

    barrier = pltpu.get_barrier_semaphore()

    def greet(i, carry):
        pl.semaphore_signal(barrier, inc=1, device_id=plane_peer(i)[1])
        return carry

    lax.fori_loop(0, 31, greet, 0)
    for d in (1, -1, 2, -2, 3, -3, 4, -4):
        pl.semaphore_signal(barrier, inc=1, device_id=at_z(z + d))

    loads = [
        pltpu.make_async_copy(src, dst, load_sem.at[i])
        for i, (src, dst) in enumerate(
            ((owner_hbm, owner), (listing_hbm, listing), (assign_hbm, assign), (emb_hbm, emb), (old_hbm, old))
        )
    ]
    for load in loads:
        load.start()
    loads[0].wait()
    loads[1].wait()

    slot_row, line_row = slot_rows(listing[...], owner[...])
    slot_col = column_of(slot_row, 256)
    loads[2].wait()
    row_slot = jnp.sum(
        jnp.where(assign[...] == iota((256, 512), 0), slot_col, 0), axis=0, keepdims=True
    )
    index = iota((512, 1), 0)
    quarter = (index >> 2) & 3
    wanted = ((index >> 4) << 2 | (index & 3)) + 1
    member_f = jnp.where(row_slot == wanted, 1.0, 0.0)
    count = jnp.sum(member_f, axis=1, keepdims=True)
    member_b = member_f.astype(BF16)
    line = jnp.sum(jnp.where(slot_row == wanted, line_row + 1, 0), axis=1, keepdims=True) - 1
    lane = iota((512, 128), 1)
    mark = jnp.where(((lane & 7) == line) & ((lane >> 3) == quarter), 1.0, 0.0)
    loads[3].wait()
    partial = jnp.zeros((512, 256), F32)
    for k in range(4):
        term = jnp.dot(member_b, emb[:, 256 * k:256 * k + 256], preferred_element_type=F32)
        partial = jnp.where(quarter == k, term, partial)
    send[:, :256], exponent = quantise(partial)
    notes = jnp.where(lane < 32, mark, jnp.where(lane < 64, count, exponent))
    send[:, 256:] = notes.astype(I32).astype(I16)

    pl.semaphore_wait(barrier, 39)

    def give(i, carry):
        t, peer = plane_peer(i)
        pltpu.make_async_remote_copy(
            src_ref=send.at[pl.ds(pl.multiple_of(t * 16, 16), 16)],
            dst_ref=recv.at[pl.ds(pl.multiple_of(me * 16, 16), 16)],
            send_sem=a2a_send,
            recv_sem=a2a_recv,
            device_id=peer,
        ).start()
        return carry

    lax.fori_loop(0, 31, give, 0)
    mine = pl.ds(pl.multiple_of(me * 16, 16), 16)
    recv[mine, :] = send[mine, :]

    k = iota((1, 512), 1)
    kc, kb, ka = k >> 8, (k >> 6) & 3, (k >> 4) & 3
    block = jnp.where(kc == 0, kb * 4 + ka, ka * 4 + kb) * 4 + ((k >> 2) & 1) * 2 + kc
    goal = ((k >> 3) & 1) * 256 + (k & 3) * 64 + block
    perm[...] = jnp.where(goal == iota((512, 512), 0), 1.0, 0.0).astype(BF16)
    out[...] = jnp.zeros_like(out)

    def all_but_one(src, dst, ssem, rsem, peer):
        return pltpu.make_async_remote_copy(
            src_ref=src.at[pl.ds(0, 496)], dst_ref=dst.at[pl.ds(0, 496)],
            send_sem=ssem, recv_sem=rsem, device_id=peer,
        )

    whole = all_but_one(send, recv, a2a_send, a2a_recv, plane_peer(0)[1])
    whole.wait_recv()
    notes = recv[:, 256:].astype(I32).astype(F32)
    marks = jnp.where(lane < 32, notes, 0.0)
    scaled = (marks * jnp.exp2(notes[:, 64:65])).astype(BF16)
    marks = marks.astype(BF16)

    def gathered(weights, values):
        return lax.dot_general(
            weights, values, (((0,), (0,)), ((), ())), preferred_element_type=F32
        )[:32]

    high, low = split2(recv[:, :256].astype(I32).astype(F32))
    total = gathered(scaled, high) + gathered(scaled, low)
    high, low = split2(notes)
    tally = (gathered(marks, high) + gathered(marks, low))[:16, 32:33]
    loads[4].wait()
    line8 = iota((8, 1), 0)
    parts = []
    for k in range(4):
        part = total[8 * k:8 * k + 8]
        for j in range(4):
            part = part + jnp.where(line8 == zh * 4 + j, old[j:j + 1, 256 * k:256 * k + 256], 0.0)
        parts.append(part)
    sums = jnp.concatenate(
        [jnp.concatenate(parts[:2], axis=1), jnp.concatenate(parts[2:], axis=1)], axis=0
    )
    zsend[:, :512], exponent = quantise(sums)
    notes = jnp.where(iota((16, 128), 1) < 64, tally, exponent)
    zsend[:, 512:] = notes.astype(I32).astype(I16)

    across = [
        pltpu.make_async_remote_copy(
            src_ref=zsend, dst_ref=zrecv.at[i], send_sem=zx_send.at[i], recv_sem=zx_recv.at[i],
            device_id=at_z(z + d),
        )
        for i, d in enumerate((4, -4))
    ]
    for move in across:
        move.start()
    for move in across:
        move.wait_recv()
    sums = jnp.zeros((16, 512), F32)
    tally = jnp.zeros((16, 1), F32)
    for i in range(2):
        notes = zrecv[i, :, 512:].astype(I32).astype(F32)
        sums = sums + zrecv[i, :, :512].astype(I32).astype(F32) * jnp.exp2(notes[:, 64:65])
        tally = tally + notes[:, :1]
    updated = sums / (tally + 1.0)
    squares = jnp.sum(updated * updated, axis=1, keepdims=True)
    mean = (squares[:8] + squares[8:]) * (1.0 / 1024)
    scale = lax.rsqrt(mean + 1e-05)
    raw[c, 0, b, a] = (updated * jnp.concatenate([scale, scale], axis=0)).astype(BF16)

    def copy(ref, sem, peer):
        return pltpu.make_async_remote_copy(
            src_ref=ref, dst_ref=ref, send_sem=ag_send, recv_sem=sem, device_id=peer
        )

    sibling = {"member": m + 1 - 2 * c}

    def z_piece(n):
        return pltpu.make_async_remote_copy(
            src_ref=raw.at[c, 0, b, a], dst_ref=raw.at[c, n, b, a],
            send_sem=ag_send, recv_sem=z_recv.at[n], device_id=at_z(z - OFFSETS[n]),
        )

    for n in (1, 2, 3, 4, 5, 6, 7):
        z_piece(n).start()

    def along_a(k, i, back):
        lo, hi = BATCHES[k]
        aa = (a + 4 - i) % 4 if back else a
        return copy(raw.at[c, lo:hi, b, aa], a_recv.at[k, i], at_plane(c, b, (a + i) % 4))

    def along_b(k, i, back):
        lo, hi = BATCHES[k]
        if lo == 1:
            lo, hi = (lo + 1, hi) if i == 1 else (lo, hi - 1)
        bb = (b + 4 - i) % 4 if back else b
        return copy(raw.at[c, lo:hi, bb], b_recv.at[k, i], at_plane(c, (b + i) % 4, a))

    def from_z(n, j):
        source, dz, near = SIDE[n]
        chunk = (b + (2, near)[j]) % 4
        return pltpu.make_async_remote_copy(
            src_ref=raw.at[c, source, chunk], dst_ref=raw.at[c, n, chunk],
            send_sem=ag_send, recv_sem=side_recv.at[n, j], device_id=at_z(z + dz),
        )

    def across_cores(n, core):
        return copy(raw.at[core, n], core_recv.at[n], sibling)

    def stage_z(k):
        for n in range(*BATCHES[k]):
            if n:
                z_piece(n).wait_recv()
        for i in (2, 1, 3):
            along_a(k, i, False).start()

    def peers_of(k):
        return (1, 3) if BATCHES[k][0] == 1 else (2, 1, 3)

    def stage_a(k):
        for i in (1, 3, 2):
            along_a(k, i, True).wait_recv()
        for i in peers_of(k):
            along_b(k, i, False).start()

    def stage_b(k):
        for i in reversed(peers_of(k)):
            along_b(k, i, True).wait_recv()
        for n in range(*BATCHES[k]):
            for target in SIDE:
                if SIDE[target][0] == n:
                    from_z(target, 0).start()
                    from_z(target, 1).start()
        for n in range(*BATCHES[k]):
            if n in SIDE:
                from_z(n, 0).wait_recv()
                from_z(n, 1).wait_recv()
            across_cores(n, c).start()

    def one_group(n, carry):
        offset = jnp.where(n % 2 == 1, (n + 1) // 2, -(n // 2))
        gg = (z + offset + 20) % 8
        first = raw[0, n].reshape(256, 512)
        second = raw[1, n].reshape(256, 512)
        for h in range(2):
            rows = slice(256 * h, 256 * h + 256)
            turned = jnp.dot(perm[rows, :256], first, preferred_element_type=F32)
            turned = turned + jnp.dot(perm[rows, 256:], second, preferred_element_type=F32)
            slab[:, 512 * h:512 * h + 512] = turned.astype(BF16)
        lanes = pl.ds(pl.multiple_of((gg // 2) * 128, 128), 128)
        for r in range(0, 512, 256):
            sim = lax.dot_general(
                emb[r:r + 256, :], slab[...], (((1,), (1,)), ((), ())), preferred_element_type=F32
            )
            best = jnp.maximum(sim[:, :128], sim[:, 128:])
            best = jnp.maximum(best, pltpu.roll(best, 64, 1)) * (1.0 / math.sqrt(1024))
            keep = (iota((256, 128), 1) >> 6) == gg % 2
            out[r:r + 256, lanes] = jnp.where(keep, best, out[r:r + 256, lanes])
        return carry

    def stage_dot(k):
        def piece(n, carry):
            across_cores(n, 1 - c).wait_recv()
            return one_group(n, carry)

        lax.fori_loop(*BATCHES[k], piece, 0)

    stage_z(0)
    stage_z(1)
    stage_z(2)
    stage_a(0)
    stage_z(3)
    stage_z(4)
    own = raw[c, 7, b, a].astype(F32)
    for h in range(2):
        part = own[8 * h:8 * h + 8]
        cent_out[:, 512 * h:512 * h + 512] = jnp.where(zh == 0, part[:4], part[4:]).astype(BF16)
    stage_a(1)
    stage_b(0)
    stage_a(2)
    stage_a(3)
    stage_a(4)
    stage_dot(0)
    stage_b(1)
    stage_b(2)
    stage_dot(1)
    stage_b(3)
    stage_dot(2)
    stage_b(4)
    stage_dot(3)
    stage_dot(4)

    whole.wait_send()
    for move in across:
        move.wait_send()
    sent = raw.reshape(4096, 512).at[pl.ds(0, 255 * 16)]
    copy(sent, z_recv.at[0], sibling).wait_send()


def shards(embeddings, assign, cluster_list, owner_map, old_centroids):
    vmem = pl.BlockSpec(memory_space=pltpu.VMEM)
    return pl.pallas_call(
        kernel,
        out_shape=(
            pltpu.VMEM((4, 1024), BF16),
            pltpu.VMEM((512, 512), F32),
        ),
        in_specs=[pl.BlockSpec(memory_space=pl.ANY)] * 5,
        out_specs=(vmem, vmem),
        scratch_shapes=[
            pltpu.VMEM((512, 1024), BF16),
            pltpu.VMEM((1, 512), I32),
            pltpu.VMEM((1, 64), I32),
            pltpu.VMEM((1, 256), I32),
            pltpu.VMEM((4, 1024), F32),
            pltpu.VMEM((512, 512), BF16),
            pltpu.VMEM((512, MSG), I16),
            pltpu.VMEM((512, MSG), I16),
            pltpu.VMEM((16, ZMSG), I16),
            pltpu.VMEM((2, 16, ZMSG), I16),
            pltpu.VMEM((2, 8, 4, 4, 16, 512), BF16),
            pltpu.VMEM((256, 1024), BF16),
            pltpu.SemaphoreType.DMA((5,)),
            pltpu.SemaphoreType.DMA,
            pltpu.SemaphoreType.DMA,
            pltpu.SemaphoreType.DMA((2,)),
            pltpu.SemaphoreType.DMA((2,)),
            pltpu.SemaphoreType.DMA,
            pltpu.SemaphoreType.DMA((8,)),
            pltpu.SemaphoreType.DMA((5, 4)),
            pltpu.SemaphoreType.DMA((5, 4)),
            pltpu.SemaphoreType.DMA((8, 2)),
            pltpu.SemaphoreType.DMA((8,)),
        ],
        compiler_params=pltpu.CompilerParams(
            collective_id=0, has_side_effects=True, vmem_limit_bytes=60 * 1024 * 1024
        ),
    )(embeddings, assign.reshape(1, -1), cluster_list, owner_map, old_centroids)


def solution(mesh):
    rows = P(("group", "member"), None)
    return jax.shard_map(
        shards,
        mesh=mesh,
        in_specs=(rows, P(("group", "member")), rows, P("group", None), rows),
        out_specs=(rows, rows),
        check_vma=False,
    )
```

```python
import math

import jax
import jax.numpy as jnp
from jax import lax
from jax.experimental import pallas as pl
from jax.experimental.pallas import tpu as pltpu
from jax.sharding import PartitionSpec as P

F32, BF16, I32, I16 = jnp.float32, jnp.bfloat16, jnp.int32, jnp.int16
MSG = 384
ZMSG = 640
OFFSETS = (0, 1, -1, 2, -2, 3, -3, 4)
SIDE = {1: (0, -1, 3), 2: (0, 1, 1)}
BATCHES = ((0, 1), (1, 3), (3, 5), (5, 7), (7, 8))


def iota(shape, dim):
    return lax.broadcasted_iota(I32, shape, dim)


def split2(v):
    high = v.astype(BF16)
    return high, (v - high.astype(F32)).astype(BF16)


def quantise(v):
    top = jnp.maximum(jnp.max(jnp.abs(v), axis=1, keepdims=True), 1e-30)
    exponent = jnp.ceil(jnp.log2(top * (1.0 / 32000)))
    return jnp.floor(v * jnp.exp2(-exponent) + 0.5).astype(I32).astype(I16), exponent


def column_of(row, n):
    eye = iota((n, n), 0) == iota((n, n), 1)
    return jnp.sum(jnp.where(eye, row, 0), axis=1, keepdims=True)


def row_of(col, n):
    eye = iota((n, n), 0) == iota((n, n), 1)
    return jnp.sum(jnp.where(eye, col, 0), axis=0, keepdims=True)


def slot_rows(list_row, pos_row):
    lists = list_row.shape[1]
    listed = jnp.max(
        jnp.where(list_row == iota((256, lists), 0), 1, 0), axis=1, keepdims=True
    )
    pos_col = column_of(pos_row, 256)
    key = jnp.where(listed > 0, pos_col, -8)
    rank = jnp.sum(
        jnp.where(((key >> 2) == (pos_row >> 2)) & (key < pos_row), 1, 0), axis=0, keepdims=True
    )
    listed_row = row_of(listed, 256)
    chip = pos_row >> 4
    core = (pos_row >> 2) & 1
    high = (pos_row >> 3) & 1
    turned = ((chip & 3) << 2) | (chip >> 2)
    target = core * 16 + jnp.where(core == 0, chip, turned)
    slot = jnp.where(listed_row > 0, target * 4 + high * 2 + rank + 1, 0)
    return slot, high * 4 + (pos_row & 3)


def kernel(
    emb_hbm, assign_hbm, listing_hbm, owner_hbm, old_hbm, cent_out, out,
    emb, assign, listing, owner, old,
    perm, send, recv, zsend, zrecv, raw, slab,
    load_sem, a2a_send, a2a_recv, zx_send, zx_recv, ag_send, z_recv, a_recv, b_recv, side_recv, core_recv,
):
    g = lax.axis_index("group")
    m = lax.axis_index("member")
    x, y, zh, c = m // 16, (m // 4) % 4, (m // 2) % 2, m % 2
    z = zh * 8 + g
    a = jnp.where(c == 0, y, x)
    b = jnp.where(c == 0, x, y)
    me = c * 16 + b * 4 + a

    def at_plane(core, bb, aa):
        xx = jnp.where(core == 0, bb, aa)
        yy = jnp.where(core == 0, aa, bb)
        return {"member": xx * 16 + yy * 4 + zh * 2 + core}

    def at_z(zz):
        zz = (zz + 16) % 16
        return {"group": zz % 8, "member": x * 16 + y * 4 + (zz // 8) * 2 + c}

    def plane_peer(i):
        def step(j):
            return jnp.where(j == 0, 2, jnp.where(j == 1, 1, jnp.where(j == 2, 3, 0)))

        xx = (x + step(i // 8)) % 4
        yy = (y + step((i // 2) % 4)) % 4
        core = (c + i + 1) % 2
        t = core * 16 + jnp.where(core == 0, xx * 4 + yy, yy * 4 + xx)
        return t, {"member": xx * 16 + yy * 4 + zh * 2 + core}

    barrier = pltpu.get_barrier_semaphore()

    def greet(i, carry):
        pl.semaphore_signal(barrier, inc=1, device_id=plane_peer(i)[1])
        return carry

    lax.fori_loop(0, 31, greet, 0)
    for d in (1, -1, 2, -2, 3, -3, 4, -4):
        pl.semaphore_signal(barrier, inc=1, device_id=at_z(z + d))

    loads = [
        pltpu.make_async_copy(src, dst, load_sem.at[i])
        for i, (src, dst) in enumerate(
            ((owner_hbm, owner), (listing_hbm, listing), (assign_hbm, assign), (emb_hbm, emb), (old_hbm, old))
        )
    ]
    for load in loads:
        load.start()
    loads[0].wait()
    loads[1].wait()

    slot_row, line_row = slot_rows(listing[...], owner[...])
    slot_col = column_of(slot_row, 256)
    loads[2].wait()
    row_slot = jnp.sum(
        jnp.where(assign[...] == iota((256, 512), 0), slot_col, 0), axis=0, keepdims=True
    )
    index = iota((512, 1), 0)
    quarter = (index >> 2) & 3
    wanted = ((index >> 4) << 2 | (index & 3)) + 1
    member_f = jnp.where(row_slot == wanted, 1.0, 0.0)
    count = jnp.sum(member_f, axis=1, keepdims=True)
    member_b = member_f.astype(BF16)
    line = jnp.sum(jnp.where(slot_row == wanted, line_row + 1, 0), axis=1, keepdims=True) - 1
    lane = iota((512, 128), 1)
    mark = jnp.where(((lane & 7) == line) & ((lane >> 3) == quarter), 1.0, 0.0)
    loads[3].wait()
    partial = jnp.zeros((512, 256), F32)
    for k in range(4):
        term = jnp.dot(member_b, emb[:, 256 * k:256 * k + 256], preferred_element_type=F32)
        partial = jnp.where(quarter == k, term, partial)
    send[:, :256], exponent = quantise(partial)
    notes = jnp.where(lane < 32, mark, jnp.where(lane < 64, count, exponent))
    send[:, 256:] = notes.astype(I32).astype(I16)

    pl.semaphore_wait(barrier, 39)

    def give(i, carry):
        t, peer = plane_peer(i)
        pltpu.make_async_remote_copy(
            src_ref=send.at[pl.ds(pl.multiple_of(t * 16, 16), 16)],
            dst_ref=recv.at[pl.ds(pl.multiple_of(me * 16, 16), 16)],
            send_sem=a2a_send,
            recv_sem=a2a_recv,
            device_id=peer,
        ).start()
        return carry

    lax.fori_loop(0, 31, give, 0)
    mine = pl.ds(pl.multiple_of(me * 16, 16), 16)
    recv[mine, :] = send[mine, :]

    k = iota((1, 512), 1)
    kc, kb, ka = k >> 8, (k >> 6) & 3, (k >> 4) & 3
    block = jnp.where(kc == 0, kb * 4 + ka, ka * 4 + kb) * 4 + ((k >> 2) & 1) * 2 + kc
    goal = ((k >> 3) & 1) * 256 + (k & 3) * 64 + block
    perm[...] = jnp.where(goal == iota((512, 512), 0), 1.0, 0.0).astype(BF16)
    out[...] = jnp.zeros_like(out)

    def all_but_one(src, dst, ssem, rsem, peer):
        return pltpu.make_async_remote_copy(
            src_ref=src.at[pl.ds(0, 496)], dst_ref=dst.at[pl.ds(0, 496)],
            send_sem=ssem, recv_sem=rsem, device_id=peer,
        )

    whole = all_but_one(send, recv, a2a_send, a2a_recv, plane_peer(0)[1])
    whole.wait_recv()
    notes = recv[:, 256:].astype(I32).astype(F32)
    marks = jnp.where(lane < 32, notes, 0.0)
    scaled = (marks * jnp.exp2(notes[:, 64:65])).astype(BF16)
    marks = marks.astype(BF16)

    def gathered(weights, values):
        return lax.dot_general(
            weights, values, (((0,), (0,)), ((), ())), preferred_element_type=F32
        )[:32]

    high, low = split2(recv[:, :256].astype(I32).astype(F32))
    total = gathered(scaled, high) + gathered(scaled, low)
    high, low = split2(notes)
    tally = (gathered(marks, high) + gathered(marks, low))[:16, 32:33]
    loads[4].wait()
    line8 = iota((8, 1), 0)
    parts = []
    for k in range(4):
        part = total[8 * k:8 * k + 8]
        for j in range(4):
            part = part + jnp.where(line8 == zh * 4 + j, old[j:j + 1, 256 * k:256 * k + 256], 0.0)
        parts.append(part)
    sums = jnp.concatenate(
        [jnp.concatenate(parts[:2], axis=1), jnp.concatenate(parts[2:], axis=1)], axis=0
    )
    zsend[:, :512], exponent = quantise(sums)
    notes = jnp.where(iota((16, 128), 1) < 64, tally, exponent)
    zsend[:, 512:] = notes.astype(I32).astype(I16)

    across = [
        pltpu.make_async_remote_copy(
            src_ref=zsend, dst_ref=zrecv.at[i], send_sem=zx_send.at[i], recv_sem=zx_recv.at[i],
            device_id=at_z(z + d),
        )
        for i, d in enumerate((4, -4))
    ]
    for move in across:
        move.start()
    for move in across:
        move.wait_recv()
    sums = jnp.zeros((16, 512), F32)
    tally = jnp.zeros((16, 1), F32)
    for i in range(2):
        notes = zrecv[i, :, 512:].astype(I32).astype(F32)
        sums = sums + zrecv[i, :, :512].astype(I32).astype(F32) * jnp.exp2(notes[:, 64:65])
        tally = tally + notes[:, :1]
    updated = sums / (tally + 1.0)
    squares = jnp.sum(updated * updated, axis=1, keepdims=True)
    mean = (squares[:8] + squares[8:]) * (1.0 / 1024)
    scale = lax.rsqrt(mean + 1e-05)
    raw[c, 0, b, a] = (updated * jnp.concatenate([scale, scale], axis=0)).astype(BF16)

    def copy(ref, sem, peer):
        return pltpu.make_async_remote_copy(
            src_ref=ref, dst_ref=ref, send_sem=ag_send, recv_sem=sem, device_id=peer
        )

    sibling = {"member": m + 1 - 2 * c}

    def z_piece(n):
        return pltpu.make_async_remote_copy(
            src_ref=raw.at[c, 0, b, a], dst_ref=raw.at[c, n, b, a],
            send_sem=ag_send, recv_sem=z_recv.at[n], device_id=at_z(z - OFFSETS[n]),
        )

    for n in (1, 2, 3, 4, 5, 6, 7):
        z_piece(n).start()

    def along_a(k, i, back):
        lo, hi = BATCHES[k]
        aa = (a + 4 - i) % 4 if back else a
        return copy(raw.at[c, lo:hi, b, aa], a_recv.at[k, i], at_plane(c, b, (a + i) % 4))

    def along_b(k, i, back):
        lo, hi = BATCHES[k]
        if lo == 1:
            lo, hi = (lo + 1, hi) if i == 1 else (lo, hi - 1)
        bb = (b + 4 - i) % 4 if back else b
        return copy(raw.at[c, lo:hi, bb], b_recv.at[k, i], at_plane(c, (b + i) % 4, a))

    def from_z(n, j):
        source, dz, near = SIDE[n]
        chunk = (b + (2, near)[j]) % 4
        return pltpu.make_async_remote_copy(
            src_ref=raw.at[c, source, chunk], dst_ref=raw.at[c, n, chunk],
            send_sem=ag_send, recv_sem=side_recv.at[n, j], device_id=at_z(z + dz),
        )

    def across_cores(n, core):
        return copy(raw.at[core, n], core_recv.at[n], sibling)

    def stage_z(k):
        for n in range(*BATCHES[k]):
            if n:
                z_piece(n).wait_recv()
        for i in (2, 1, 3):
            along_a(k, i, False).start()

    def peers_of(k):
        return (1, 3) if BATCHES[k][0] == 1 else (2, 1, 3)

    def stage_a(k):
        for i in (1, 3, 2):
            along_a(k, i, True).wait_recv()
        for i in peers_of(k):
            along_b(k, i, False).start()

    def stage_b(k):
        for i in reversed(peers_of(k)):
            along_b(k, i, True).wait_recv()
        for n in range(*BATCHES[k]):
            for target in SIDE:
                if SIDE[target][0] == n:
                    from_z(target, 0).start()
                    from_z(target, 1).start()
        for n in range(*BATCHES[k]):
            if n in SIDE:
                from_z(n, 0).wait_recv()
                from_z(n, 1).wait_recv()
            across_cores(n, c).start()

    def one_group(n, carry):
        offset = jnp.where(n % 2 == 1, (n + 1) // 2, -(n // 2))
        gg = (z + offset + 20) % 8
        both = jnp.concatenate([raw[0, n].reshape(256, 512), raw[1, n].reshape(256, 512)], axis=0)
        for h in range(2):
            rows = slice(256 * h, 256 * h + 256)
            turned = jnp.dot(perm[rows, :], both, preferred_element_type=F32)
            slab[:, 512 * h:512 * h + 512] = turned.astype(BF16)
        lanes = pl.ds(pl.multiple_of((gg // 2) * 128, 128), 128)
        for r in range(0, 512, 256):
            sim = lax.dot_general(
                emb[r:r + 256, :], slab[...], (((1,), (1,)), ((), ())), preferred_element_type=F32
            )
            best = jnp.maximum(sim[:, :128], sim[:, 128:])
            best = jnp.maximum(best, pltpu.roll(best, 64, 1)) * (1.0 / math.sqrt(1024))
            keep = (iota((256, 128), 1) >> 6) == gg % 2
            out[r:r + 256, lanes] = jnp.where(keep, best, out[r:r + 256, lanes])
        return carry

    def stage_dot(k):
        def piece(n, carry):
            across_cores(n, 1 - c).wait_recv()
            return one_group(n, carry)

        lax.fori_loop(*BATCHES[k], piece, 0)

    stage_z(0)
    stage_z(1)
    stage_z(2)
    stage_a(0)
    stage_z(3)
    stage_z(4)
    own = raw[c, 7, b, a].astype(F32)
    for h in range(2):
        part = own[8 * h:8 * h + 8]
        cent_out[:, 512 * h:512 * h + 512] = jnp.where(zh == 0, part[:4], part[4:]).astype(BF16)
    stage_a(1)
    stage_b(0)
    stage_a(2)
    stage_a(3)
    stage_a(4)
    stage_dot(0)
    stage_b(1)
    stage_b(2)
    stage_dot(1)
    stage_b(3)
    stage_dot(2)
    stage_b(4)
    stage_dot(3)
    stage_dot(4)

    whole.wait_send()
    for move in across:
        move.wait_send()
    sent = raw.reshape(4096, 512).at[pl.ds(0, 255 * 16)]
    copy(sent, z_recv.at[0], sibling).wait_send()


def shards(embeddings, assign, cluster_list, owner_map, old_centroids):
    vmem = pl.BlockSpec(memory_space=pltpu.VMEM)
    return pl.pallas_call(
        kernel,
        out_shape=(
            pltpu.VMEM((4, 1024), BF16),
            pltpu.VMEM((512, 512), F32),
        ),
        in_specs=[pl.BlockSpec(memory_space=pl.ANY)] * 5,
        out_specs=(vmem, vmem),
        scratch_shapes=[
            pltpu.VMEM((512, 1024), BF16),
            pltpu.VMEM((1, 512), I32),
            pltpu.VMEM((1, 64), I32),
            pltpu.VMEM((1, 256), I32),
            pltpu.VMEM((4, 1024), F32),
            pltpu.VMEM((512, 512), BF16),
            pltpu.VMEM((512, MSG), I16),
            pltpu.VMEM((512, MSG), I16),
            pltpu.VMEM((16, ZMSG), I16),
            pltpu.VMEM((2, 16, ZMSG), I16),
            pltpu.VMEM((2, 8, 4, 4, 16, 512), BF16),
            pltpu.VMEM((256, 1024), BF16),
            pltpu.SemaphoreType.DMA((5,)),
            pltpu.SemaphoreType.DMA,
            pltpu.SemaphoreType.DMA,
            pltpu.SemaphoreType.DMA((2,)),
            pltpu.SemaphoreType.DMA((2,)),
            pltpu.SemaphoreType.DMA,
            pltpu.SemaphoreType.DMA((8,)),
            pltpu.SemaphoreType.DMA((5, 4)),
            pltpu.SemaphoreType.DMA((5, 4)),
            pltpu.SemaphoreType.DMA((8, 2)),
            pltpu.SemaphoreType.DMA((8,)),
        ],
        compiler_params=pltpu.CompilerParams(
            collective_id=0, has_side_effects=True, vmem_limit_bytes=60 * 1024 * 1024
        ),
    )(embeddings, assign.reshape(1, -1), cluster_list, owner_map, old_centroids)


def solution(mesh):
    rows = P(("group", "member"), None)
    return jax.shard_map(
        shards,
        mesh=mesh,
        in_specs=(rows, P(("group", "member")), rows, P("group", None), rows),
        out_specs=(rows, rows),
        check_vma=False,
    )
```
